32 devices in a mesh: cluster: 4 (over y, x), sub: 8 (over z, core).
Axes of the slice: x: 2, y: 2, z: 4, core: 2. Of those that a mesh axis runs over, the one named last changes fastest.
Arguments:
- dual_ops: float32 [4, 8, 1408, 1408], P('cluster', 'sub'), may hold values from -1 to 4.5, as said below
- contributions: float32 [4, 8, 1408, 64], P('cluster', 'sub'), may hold values from -6 to 6
- block_sizes: int32 [4, 8, 4], P('cluster', 'sub'), may hold values from 0 to 352, as said below
- mult_map: int32 [4, 8, 1408], P('cluster', 'sub'), may hold values from 0 to 1407, each once within a row
- coarse_basis: float32 [4, 8, 32, 704], P('cluster', 'sub'), may hold values from -0.21875 to 0.21875
- coarse_inverse: float32 [4, 256, 256], P('cluster'), may hold values from -0.1 to 0.5, as said below
Outputs:
- solution: float32 [4, 8, 1408, 64], P('cluster', 'sub')
- residual: float32 [4, 8, 1408, 64], P('cluster', 'sub')
The draws below stay inside these ranges and needn't reach their ends.
Inputs may be any that keep to these rules, and one draw needn't show every extreme that they name: `dual_ops`: symmetric positive definite for each subdomain. block_sizes[c, s, k] equals the count on the facing side of the neighbour across side k; sides at the ends of an axis hold 0, all others 352 // 4 to 352; some side holds exactly 352. `mult_map`: for each subdomain a permutation of the 1408 slots. `coarse_inverse`: symmetric for each cluster.
All inputs are finite; a program needn't handle non-finite values.
Results may differ from the reference program's by a relative error of at most 0.0003.
Values sent between devices are 32-bit elements; how exact they have to be, the bound alone decides.
No kernel may reach another device: no remote copies, remote signals or barrier semaphores. Data moves between devices by JAX's collectives and lax.ppermute only.
A program may use at most 64 MiB of HBM per device.

```python
import math
import jax
import jax.numpy as jnp
from jax import lax

M = 1408
PAD = 352
MODES = 32
R = 64
ITERS = 2
CLUSTERS = 4
SUBS = 8
COARSE = 256


def one_operator(subkey):
    first_key, second_key = jax.random.split(subkey)
    noise_matrix = jax.random.normal(first_key, (M, M), jnp.float32)
    diagonal_values = jnp.exp(jax.random.uniform(second_key, (M,), jnp.float32, math.log(1.2), math.log(3.6)))
    return (noise_matrix + noise_matrix.T) * (1.0 / (2.8 * math.sqrt(M))) + jnp.diag(diagonal_values)


def draw_dual_ops(key, part):
    subkeys = jax.random.split(jax.random.fold_in(key, 7), CLUSTERS * SUBS)
    return lax.map(one_operator, subkeys).reshape(CLUSTERS, SUBS, M, M)


def draw_block_sizes(key, part):
    first_key, second_key = jax.random.split(jax.random.fold_in(key, 11))
    sub_edges = jax.random.randint(first_key, (CLUSTERS, SUBS - 1), PAD // 4, PAD + 1).astype(jnp.int32)
    sub_edges = sub_edges.at[0, 0].set(PAD)
    cluster_edges = jax.random.randint(second_key, (CLUSTERS - 1, SUBS), PAD // 4, PAD + 1).astype(jnp.int32)
    zero_column = jnp.zeros((CLUSTERS, 1), jnp.int32)
    zero_line = jnp.zeros((1, SUBS), jnp.int32)
    west_side = jnp.concatenate([zero_column, sub_edges], axis=1)
    east_side = jnp.concatenate([sub_edges, zero_column], axis=1)
    south_side = jnp.concatenate([zero_line, cluster_edges], axis=0)
    north_side = jnp.concatenate([cluster_edges, zero_line], axis=0)
    return jnp.stack([west_side, east_side, south_side, north_side], axis=-1).astype(jnp.int32)


def draw_coarse_inverse(key, part):
    first_key, second_key = jax.random.split(jax.random.fold_in(key, 13))
    noise_matrix = jax.random.normal(first_key, (CLUSTERS, COARSE, COARSE), jnp.float32)
    diagonal_values = jnp.exp(jax.random.uniform(second_key, (CLUSTERS, COARSE), jnp.float32, math.log(0.1), math.log(0.3)))
    symmetric = (noise_matrix + jnp.swapaxes(noise_matrix, 1, 2)) * (0.002 / math.sqrt(2.0))
    return symmetric + diagonal_values[..., None] * jnp.eye(COARSE, dtype=jnp.float32)[None]


def level_of(own_key, dims, cuts, smallest, largest):
    def one(position, parts):
        draws = jax.random.uniform(jax.random.fold_in(jax.random.fold_in(own_key, 6), position), (parts,), jnp.float32, smallest / len(cuts), largest / len(cuts))
        return jnp.repeat(jnp.exp(draws), dims[position] // parts).reshape((-1,) + (1,) * (len(dims) - position - 1))

    level = one(*cuts[0])
    for cut in cuts[1:]:
        level = level * one(*cut)
    return level


def normal_values(stream_key, dims, scale, most, cuts=(), kind=jnp.bfloat16):
    level = level_of(stream_key, dims, cuts, -0.22, 0.18) if cuts else 1.0
    entries = jax.random.normal(stream_key, dims, jnp.float32) * scale * level
    return jnp.minimum(jnp.maximum(entries, -most), most).astype(kind)


def setup_inputs(seed: int = 0) -> dict:
    keys = jax.random.split(jax.random.key(seed), 7)
    dual_ops = draw_dual_ops(jax.random.fold_in(keys[6], 71), 0)
    contributions = normal_values(keys[1], (CLUSTERS, SUBS, M, R), 1.0, 6.0, ((0, 4), (1, 8)), jnp.float32)
    block_sizes = draw_block_sizes(jax.random.fold_in(keys[6], 71), 0)
    mult_map = jax.vmap(lambda own: jax.random.permutation(own, M))(jax.random.split(keys[3], CLUSTERS * SUBS)).reshape((CLUSTERS, SUBS, M)).astype(jnp.int32)
    coarse_basis = normal_values(keys[4], (CLUSTERS, SUBS, MODES, 2 * PAD), (2 * PAD) ** -0.5, 0.21875, ((0, 4), (1, 8)), jnp.float32)
    coarse_inverse = draw_coarse_inverse(jax.random.fold_in(keys[6], 71), 0)
    return dict(dual_ops=dual_ops, contributions=contributions, block_sizes=block_sizes, mult_map=mult_map, coarse_basis=coarse_basis, coarse_inverse=coarse_inverse)


precise = lax.Precision.HIGHEST

def slot_weights(block_sizes):
    row_index = jnp.arange(M, dtype=jnp.int32)
    row_side = row_index // PAD
    row_place = row_index % PAD
    side_match = row_side[None, None, :, None] == jnp.arange(4, dtype=jnp.int32)[None, None, None, :]
    row_limit = jnp.sum(jnp.where(side_match, block_sizes[:, :, None, :], 0), axis=3)
    live_rows = (row_place[None, None, :] < row_limit).astype(jnp.float32)[..., None]
    row_sign = jnp.where(row_side % 2 == 0, -1.0, 1.0).astype(jnp.float32)
    return (live_rows, live_rows * row_sign[None, None, :, None])

def assemble(values, live_rows, row_weight):
    blocks = (values * row_weight).reshape(CLUSTERS, SUBS, 4, PAD, R)
    west_part = blocks[:, :, 0]
    east_part = blocks[:, :, 1]
    south_part = blocks[:, :, 2]
    north_part = blocks[:, :, 3]
    zero_sub = jnp.zeros((CLUSTERS, 1, PAD, R), jnp.float32)
    zero_cluster = jnp.zeros((1, SUBS, PAD, R), jnp.float32)
    new_west = west_part + jnp.concatenate([zero_sub, east_part[:, :-1]], axis=1)
    new_east = east_part + jnp.concatenate([west_part[:, 1:], zero_sub], axis=1)
    new_south = south_part + jnp.concatenate([zero_cluster, north_part[:-1]], axis=0)
    new_north = north_part + jnp.concatenate([south_part[1:], zero_cluster], axis=0)
    joined = jnp.stack([new_west, new_east, new_south, new_north], axis=2)
    return joined.reshape(CLUSTERS, SUBS, M, R) * live_rows

def apply_dual(values, dual_ops, mult_map, inverse_map, live_rows, row_weight):
    local_vals = jnp.take_along_axis(values * row_weight, mult_map[..., None], axis=2)
    mapped = jnp.einsum('csmn,csnr->csmr', dual_ops, local_vals, precision=precise)
    return assemble(jnp.take_along_axis(mapped, inverse_map[..., None], axis=2), live_rows, row_weight)

def project(values, coarse_basis, coarse_inverse, live_rows, row_weight):
    signed = (values * row_weight)[:, :, :2 * PAD]
    moments = jnp.einsum('cskp,cspr->cskr', coarse_basis, signed, precision=precise).reshape(CLUSTERS, COARSE, R)
    coefficients = jnp.einsum('cij,cjr->cir', coarse_inverse, moments, precision=precise).reshape(CLUSTERS, SUBS, MODES, R)
    lifted = jnp.einsum('cskp,cskr->cspr', coarse_basis, coefficients, precision=precise)
    padded = jnp.concatenate([lifted, jnp.zeros((CLUSTERS, SUBS, 2 * PAD, R), jnp.float32)], axis=2)
    return values - assemble(padded, live_rows, row_weight)

def inner_product(left, right):
    return 0.5 * jnp.einsum('csmi,csmj->ij', left, right, precision=precise)

def chol_solve(factor, target):
    middle = lax.linalg.triangular_solve(factor, target, left_side=True, lower=True)
    return lax.linalg.triangular_solve(factor, middle, left_side=True, lower=True, transpose_a=True)

def times_small(vectors, small):
    return jnp.einsum('csmi,ij->csmj', vectors, small, precision=precise)

def reference(dual_ops, contributions, block_sizes, mult_map, coarse_basis, coarse_inverse):
    live_rows, row_weight = slot_weights(block_sizes)
    inverse_map = jnp.argsort(mult_map, axis=-1).astype(jnp.int32)

    def projected(values):
        return project(values, coarse_basis, coarse_inverse, live_rows, row_weight)
    residual = projected(assemble(contributions, live_rows, row_weight))
    solution = jnp.zeros_like(residual)
    direction = residual
    for iteration in range(ITERS):
        mapped = projected(apply_dual(projected(direction), dual_ops, mult_map, inverse_map, live_rows, row_weight))
        curvature = inner_product(direction, mapped)
        descent = inner_product(direction, residual)
        factor = jnp.linalg.cholesky(curvature)
        step_size = chol_solve(factor, descent)
        solution = solution + times_small(direction, step_size)
        residual = residual - times_small(mapped, step_size)
        if iteration + 1 < ITERS:
            coupling = inner_product(mapped, residual)
            direction_mix = -chol_solve(factor, coupling)
            direction = residual + times_small(direction, direction_mix)
    return (solution, residual)
```

```python
import jax
import jax.numpy as jnp
from jax import lax
from jax.sharding import PartitionSpec as P

precise = lax.Precision.HIGHEST


def dot(left, right):
    return jnp.dot(left, right, precision=precise, preferred_element_type=jnp.float32)


def dot_t(left, right):
    return lax.dot_general(
        left, right, (((0,), (0,)), ((), ())), precision=precise, preferred_element_type=jnp.float32
    )


def partners(axis, step):
    return [(i, i ^ step) for i in range(lax.axis_size(axis))]


def shift(value, axis, by):
    peers = lax.axis_size(axis)
    return lax.ppermute(value, axis, [(i, i + by) for i in range(peers) if 0 <= i + by < peers])


def gathered(value, axis):
    peers = lax.axis_size(axis)
    value = value[None]
    step = 1
    while step < peers:
        value = jnp.concatenate([value, lax.ppermute(value, axis, partners(axis, step))], axis=0)
        step *= 2
    return value


def summed(value, axis):
    step = 1
    while step < lax.axis_size(axis):
        value = value + lax.ppermute(value, axis, partners(axis, step))
        step *= 2
    return value


def spd_solve(matrix, target):
    factor = jnp.linalg.cholesky(matrix)
    middle = lax.linalg.triangular_solve(factor, target, left_side=True, lower=True)
    return lax.linalg.triangular_solve(factor, middle, left_side=True, lower=True, transpose_a=True)


def shards(dual_ops, contributions, block_sizes, mult_map, coarse_basis, coarse_inverse):
    operator, rhs, sizes, slot_map = dual_ops[0, 0], contributions[0, 0], block_sizes[0, 0], mult_map[0, 0]
    basis, coarse = coarse_basis[0, 0], coarse_inverse[0]
    order, columns = rhs.shape
    face = order // 4
    modes = basis.shape[0]
    subs = lax.axis_size("sub")
    me = lax.axis_index("sub")
    place = jnp.arange(face, dtype=jnp.int32)
    live = (place[None, :] < sizes[:, None]).astype(jnp.float32).reshape(order, 1)
    sign = jnp.repeat(jnp.array([-1.0, 1.0, -1.0, 1.0], jnp.float32), face)[:, None]
    inverse_map = jnp.argsort(slot_map)

    def jump(values):
        sides = values.reshape(4, face, columns)
        facing = jnp.stack(
            [
                shift(sides[1], "sub", 1),
                shift(sides[0], "sub", -1),
                shift(sides[3], "cluster", 1),
                shift(sides[2], "cluster", -1),
            ]
        ).reshape(order, columns)
        return (values - facing) * live

    def operate(values):
        return jnp.take(dot(operator, jnp.take(values, slot_map, axis=0)), inverse_map, axis=0)

    left = shift(basis[:, face:], "sub", 1)
    right = shift(basis[:, :face], "sub", -1)
    zero = jnp.zeros_like(left)
    modes_near = jnp.concatenate(
        [
            jnp.concatenate([-left, zero], axis=1),
            basis,
            jnp.concatenate([zero, -right], axis=1),
        ],
        axis=0,
    ) * live[: 2 * face, 0][None, :]
    own_modes = modes_near[modes : 2 * modes]

    padded = jnp.pad(coarse, ((modes, modes), (0, 0)))
    near_rows = lax.dynamic_slice_in_dim(padded, me * modes, 3 * modes, 0)

    v0 = jump(rhs)
    packet = jnp.concatenate([dot(own_modes, v0[: 2 * face]), dot(own_modes, modes_near.T)], axis=1)
    packets = gathered(packet, "sub")
    natural = packets[jnp.arange(subs) ^ me]
    m0 = natural[:, :, :columns].reshape(subs * modes, columns)
    blocks = natural[:, :, columns:]
    near_inverse = jnp.stack([padded[j * modes : (j + 3) * modes] for j in range(subs)])
    t_c = lax.dot_general(
        blocks, near_inverse, (((2,), (1,)), ((0,), (0,))), precision=precise, preferred_element_type=jnp.float32
    ).reshape(subs * modes, subs * modes)
    twice_rows = 2.0 * near_rows - dot(near_rows, t_c)

    def corrected(values, coefficients):
        return values.at[: 2 * face].add(-dot_t(modes_near, coefficients))

    def near_sum(parts):
        total = jnp.zeros(((subs + 2) * modes, columns), jnp.float32)
        parts = parts[jnp.arange(subs) ^ me]
        for j in range(subs):
            total = total.at[j * modes : (j + 3) * modes].add(parts[j])
        return total[modes:-modes]

    r0 = corrected(v0, dot(near_rows, m0))
    u0 = corrected(v0, dot(twice_rows, m0))
    y1 = operate(u0)
    v1 = jump(y1)
    m1 = near_sum(gathered(dot(modes_near, y1[: 2 * face]), "sub"))
    h1 = corrected(v1, dot(near_rows, m1))
    u1 = corrected(v1, dot(twice_rows, m1))
    y2 = operate(u1)
    v2 = jump(y2)
    m2 = near_sum(gathered(dot(modes_near, y2[: 2 * face]), "sub"))
    h2 = corrected(v2, dot(near_rows, m2))
    grams = jnp.stack([0.5 * dot_t(r0, r0), dot_t(u0, y1), 0.5 * dot_t(h1, h1), dot_t(u1, y2)])
    g0, g1, g2, g3 = summed(summed(grams, "sub"), "cluster")
    both = spd_solve(g1, jnp.concatenate([g0, g2], axis=1))
    first, mix = both[:, :columns], both[:, columns:]
    last = spd_solve(g3 - dot(g2, mix), dot(g2, first) - g1)
    alpha = first + dot(mix, last)
    answer = (dot(r0, alpha) - dot(h1, last)) * sign
    rest = (r0 - dot(h1, alpha) + dot(h2, last)) * sign
    return answer[None, None], rest[None, None]


def solution(mesh):
    return jax.shard_map(
        shards,
        mesh=mesh,
        in_specs=(
            P("cluster", "sub", None, None),
            P("cluster", "sub", None, None),
            P("cluster", "sub", None),
            P("cluster", "sub", None),
            P("cluster", "sub", None, None),
            P("cluster", None, None),
        ),
        out_specs=(P("cluster", "sub", None, None), P("cluster", "sub", None, None)),
        check_vma=False,
    )
```

```python
import functools

import jax
import jax.numpy as jnp
from jax import lax
from jax.experimental import pallas as pl
from jax.experimental.pallas import tpu as pltpu
from jax.sharding import PartitionSpec as P

F32 = jnp.float32
BF16 = jnp.bfloat16


def contract(left, right, dims):
    return lax.dot_general(
        left, right, ((dims[0], dims[1]), ((), ())), precision=lax.Precision.HIGHEST, preferred_element_type=F32
    )


def matmul(left, right):
    return contract(left, right, ((1,), (0,)))


def matmul_tn(left, right):
    return contract(left, right, ((0,), (0,)))


def matmul_nt(left, right):
    return contract(left, right, ((1,), (1,)))


def passes(left, right):
    return jnp.dot(left, right, preferred_element_type=F32)


def pack(rows):
    half = rows.shape[0] // 2
    return jnp.concatenate([rows[:half], rows[half:]], axis=1)


def unpack(packed):
    half = packed.shape[1] // 2
    return jnp.concatenate([packed[:, :half], packed[:, half:]], axis=0)


def wide(values):
    first = values.astype(BF16).astype(F32)
    rest = values - first
    second = rest.astype(BF16).astype(F32)
    third = rest - second
    return jnp.concatenate(
        [
            jnp.concatenate([first, second], axis=1).astype(BF16),
            jnp.concatenate([third, jnp.zeros_like(third)], axis=1).astype(BF16),
        ],
        axis=1,
    )


def narrow(values):
    half = values.shape[1] // 2
    values = values[:, :half] + values[:, half:]
    half = half // 2
    return values[:, :half] + values[:, half:]


def operate(u, map_row, map_column, operator, work, y_ref, face):
    order = operator.shape[0]
    parts = wide(u)
    slots = lax.broadcasted_iota(jnp.int32, (face, order), 1)
    for begin in range(0, order, face):
        rows = slice(begin, begin + face)
        take = (map_column[rows, :] == slots).astype(F32).astype(BF16)
        work[rows, :] = passes(take, parts).astype(BF16)
    parts = work[...]
    for begin in range(0, order, face):
        rows = slice(begin, begin + face)
        block = operator[rows, :]
        high = block.astype(BF16)
        low = (block - high.astype(F32)).astype(BF16)
        work[rows, :] = wide(narrow(passes(high, parts) + passes(low, parts)))
    parts = work[...]
    slots = lax.broadcasted_iota(jnp.int32, (face, order), 0)
    for begin in range(0, order, face):
        rows = slice(begin, begin + face)
        put = (map_row[...] == slots + begin).astype(F32).astype(BF16)
        y_ref[rows, :] = narrow(passes(put, parts))


def parities(info):
    return info[4] % 2, info[5] % 2


def write_faces(info, source, outs, face):
    sub_odd, cluster_odd = parities(info)
    sides = (1 - sub_odd, sub_odd, 3 - cluster_odd, 2 + cluster_odd)
    for side, out in zip(sides, outs):
        out[: face // 2, :] = pack(source[pl.ds(pl.multiple_of(side * face, 16), face), :])


def facing_pair(odd, even_pair, odd_pair):
    return jnp.where(odd == 0, odd_pair, even_pair), jnp.where(odd == 0, even_pair, odd_pair)


def jump(info, source, packets, v_ref, face):
    sub_odd, cluster_odd = parities(info)
    half = face // 2
    halos = [packet[:half, :] for packet in packets]
    facing = facing_pair(sub_odd, halos[0], halos[1]) + facing_pair(cluster_odd, halos[2], halos[3])
    place = lax.broadcasted_iota(jnp.int32, (face, source.shape[1]), 0)
    for side in range(4):
        rows = slice(side * face, (side + 1) * face)
        v_ref[rows, :] = jnp.where(place < info[side], source[rows, :] - unpack(facing[side]), 0.0)


def start_kernel(info, rhs, basis, even_ref, odd_ref, even_cluster_ref, odd_cluster_ref):
    face = rhs.shape[0] // 4
    modes = basis.shape[0]
    write_faces(info, rhs, (even_ref, odd_ref, even_cluster_ref, odd_cluster_ref), face)
    sub_odd, _ = parities(info)
    lower, upper = basis[:, :face], basis[:, face:]
    half = face // 2
    for out, chosen in (
        (even_ref, jnp.where(sub_odd == 0, upper, lower)),
        (odd_ref, jnp.where(sub_odd == 0, lower, upper)),
    ):
        lanes = out.shape[1]
        for i, begin in enumerate(range(0, face, lanes)):
            piece = chosen[:, begin : min(begin + lanes, face)]
            if piece.shape[1] < lanes:
                piece = jnp.concatenate([piece, jnp.zeros((modes, lanes - piece.shape[1]), F32)], axis=1)
            out[half + i * modes : half + (i + 1) * modes, :] = piece


def first_kernel(info, rhs, basis, even, odd, even_cluster, odd_cluster, v_ref, near_ref, packet_ref):
    face = rhs.shape[0] // 4
    modes = basis.shape[0]
    columns = rhs.shape[1]
    half = face // 2
    jump(info, rhs, (even, odd, even_cluster, odd_cluster), v_ref, face)
    sub_odd, _ = parities(info)

    def face_modes(packet):
        pieces = [packet[half + i : half + i + modes, :] for i in range(0, packet.shape[0] - half, modes)]
        return jnp.concatenate(pieces, axis=1)[:, :face]

    left, right = facing_pair(sub_odd, face_modes(even), face_modes(odd))
    zero = jnp.zeros_like(left)
    near = jnp.concatenate(
        [
            jnp.concatenate([-left, zero], axis=1),
            basis[...],
            jnp.concatenate([zero, -right], axis=1),
        ],
        axis=0,
    )
    place = lax.broadcasted_iota(jnp.int32, near.shape, 1)
    alive = jnp.logical_or(
        place < info[0], jnp.logical_and(place >= face, place < face + info[1])
    )
    near = jnp.where(alive, near, 0.0)
    near_ref[...] = near
    own = near[modes : 2 * modes]
    packet_ref[...] = jnp.zeros_like(packet_ref)
    packet_ref[:, :columns] = matmul(own, v_ref[: 2 * face, :])
    packet_ref[:, 2 * columns : 2 * columns + 3 * modes] = matmul_nt(own, near)


def lifted(near, coefficients, modes):
    both = jnp.concatenate([coefficients[: 3 * modes], coefficients[3 * modes :]], axis=1)
    return matmul_tn(near[...], both)


def write_packets(info, near, y_ref, outs, face):
    write_faces(info, y_ref, outs, face)
    moments = matmul(near[...], y_ref[: 2 * face, :])
    outs[0][face // 2 :, :] = pack(moments)


def second_kernel(
    info, packets, coarse, near, v0, map_row, map_column, operator,
    r_ref, y_ref, even_ref, odd_ref, even_cluster_ref, odd_cluster_ref, rows_ref, gram_ref,
    natural, padded, product, work,
):
    order, columns = v0.shape
    face = order // 4
    modes = near.shape[0] // 3
    total = coarse.shape[0]
    subs = total // modes
    me = info[4]
    for j in range(subs):
        natural[pl.ds(pl.multiple_of((me ^ j) * modes, modes), modes), :] = packets[j * modes : (j + 1) * modes, :]
    padded[:modes, :] = jnp.zeros((modes, total), F32)
    padded[modes + total :, :] = jnp.zeros((modes, total), F32)
    padded[modes : modes + total, :] = coarse[...]
    for j in range(subs):
        rows = slice(j * modes, (j + 1) * modes)
        product[rows, :] = matmul(
            natural[rows, 2 * columns : 2 * columns + 3 * modes], padded[j * modes : (j + 3) * modes, :]
        )
    once = padded[pl.ds(pl.multiple_of(me * modes, modes), 3 * modes), :]
    rows_ref[: 3 * modes, :] = once
    rows_ref[3 * modes :, :] = 2.0 * once - matmul(once, product[...])
    both = lifted(near, matmul(rows_ref[...], natural[:, :columns]), modes)
    r_ref[...] = v0[...]
    r_ref[: 2 * face, :] = v0[: 2 * face, :] - both[:, :columns]
    u = jnp.concatenate([v0[: 2 * face, :] - both[:, columns:], v0[2 * face :, :]], axis=0)
    operate(u, map_row, map_column, operator, work, y_ref, face)
    write_packets(info, near, y_ref, (even_ref, odd_ref, even_cluster_ref, odd_cluster_ref), face)
    r = r_ref[...]
    gram_ref[:, :columns] = 0.5 * matmul_tn(r, r)
    gram_ref[:, columns:] = matmul_tn(u, y_ref[...])


def sum_moments(info, moments, total_ref, modes):
    subs = total_ref.shape[0] // modes - 2
    rows = 3 * modes // 2
    total_ref[...] = jnp.zeros_like(total_ref)
    for j in range(subs):
        where = pl.ds(pl.multiple_of((info[4] ^ j) * modes, modes), 3 * modes)
        total_ref[where, :] = total_ref[where, :] + unpack(moments[j * rows : (j + 1) * rows, :])
    return total_ref[modes : modes * (subs + 1), :]


def third_kernel(
    info, y1, even, odd, even_cluster, odd_cluster, moments, rows, near, map_row, map_column, operator,
    h_ref, y_ref, even_ref, odd_ref, even_cluster_ref, odd_cluster_ref, gram_ref,
    total_ref, v_ref, work,
):
    order, columns = y1.shape
    face = order // 4
    modes = near.shape[0] // 3
    jump(info, y1, (even, odd, even_cluster, odd_cluster), v_ref, face)
    both = lifted(near, matmul(rows[...], sum_moments(info, moments, total_ref, modes)), modes)
    h_ref[...] = v_ref[...]
    h_ref[: 2 * face, :] = v_ref[: 2 * face, :] - both[:, :columns]
    u = jnp.concatenate([v_ref[: 2 * face, :] - both[:, columns:], v_ref[2 * face :, :]], axis=0)
    operate(u, map_row, map_column, operator, work, y_ref, face)
    write_packets(info, near, y_ref, (even_ref, odd_ref, even_cluster_ref, odd_cluster_ref), face)
    h = h_ref[...]
    gram_ref[:, :columns] = 0.5 * matmul_tn(h, h)
    gram_ref[:, columns:] = matmul_tn(u, y_ref[...])


def spd_solve(matrix, target):
    order = matrix.shape[0]
    table = jnp.concatenate([matrix, target], axis=1)
    lines = lax.broadcasted_iota(jnp.int32, (order, 1), 0)
    scale = jnp.zeros((order, 1), F32)
    for k in range(order):
        column = table[:, k : k + 1]
        pivot = table[k : k + 1, :]
        inverse = 1.0 / table[k : k + 1, k : k + 1]
        scale = jnp.where(lines == k, inverse, scale)
        table = table - jnp.where(lines == k, 0.0, column * inverse) * pivot
    return table[:, order:] * scale


def last_kernel(
    info, y2, even, odd, even_cluster, odd_cluster, moments, rows, near, r0, h1, grams,
    solution_ref, residual_ref,
    total_ref, v_ref,
):
    order, columns = y2.shape
    face = order // 4
    modes = near.shape[0] // 3
    g = grams[...]
    g0, g1, g2, g3 = g[:columns, :columns], g[:columns, columns:], g[columns:, :columns], g[columns:, columns:]
    matrix = jnp.concatenate(
        [jnp.concatenate([g1, g2], axis=1), jnp.concatenate([g2, g3], axis=1)], axis=0
    )
    answer = spd_solve(matrix, jnp.concatenate([g0, g1], axis=0))
    alpha, negative = answer[:columns], answer[columns:]
    jump(info, y2, (even, odd, even_cluster, odd_cluster), v_ref, face)
    own = matmul(rows[: 3 * modes, :], sum_moments(info, moments, total_ref, modes))
    v_ref[: 2 * face, :] = v_ref[: 2 * face, :] - matmul_tn(near[...], own)
    zero = jnp.zeros_like(alpha)
    weights = jnp.concatenate(
        [
            jnp.concatenate([alpha, zero], axis=1),
            jnp.concatenate([negative, -alpha], axis=1),
            jnp.concatenate([zero, -negative], axis=1),
        ],
        axis=0,
    )
    for side in range(4):
        sign = 1.0 if side % 2 else -1.0
        lines = slice(side * face, (side + 1) * face)
        r = r0[lines, :]
        basis = jnp.concatenate([r, h1[lines, :], v_ref[lines, :]], axis=1)
        both = matmul(basis, weights)
        solution_ref[lines, :] = sign * both[:, :columns]
        residual_ref[lines, :] = sign * (r + both[:, columns:])


def call(kernel, name, outs, scratch, *args):
    smem = pl.BlockSpec(memory_space=pltpu.SMEM)
    vmem = pl.BlockSpec(memory_space=pltpu.VMEM)
    return pl.pallas_call(
        kernel,
        name=name,
        out_shape=[jax.ShapeDtypeStruct(shape, F32) for shape in outs],
        in_specs=[smem] + [vmem] * (len(args) - 1),
        out_specs=[vmem] * len(outs),
        scratch_shapes=scratch,
        compiler_params=pltpu.CompilerParams(vmem_limit_bytes=36 * 2**20),
    )(*args)


def pairs(value, axis, odd):
    peers = lax.axis_size(axis)
    low = [(i, i + 1) for i in range(odd, peers - 1, 2)]
    return lax.ppermute(value, axis, low + [(j, i) for i, j in low])


def swap(value, axis, step):
    return lax.ppermute(value, axis, [(i, i ^ step) for i in range(lax.axis_size(axis))])


def steps(axis, first):
    size = first
    while size < lax.axis_size(axis):
        yield size
        size *= 2


def shards(dual_ops, contributions, block_sizes, mult_map, coarse_basis, coarse_inverse):
    operator, rhs, sizes, slot_map = dual_ops[0, 0], contributions[0, 0], block_sizes[0, 0], mult_map[0, 0]
    basis, coarse = coarse_basis[0, 0], coarse_inverse[0]
    order, columns = rhs.shape
    face = order // 4
    half = face // 2
    modes = basis.shape[0]
    total = coarse.shape[0]
    lanes = 2 * columns
    mode_rows = -(-face // lanes) * modes
    moment_rows = 3 * modes // 2
    info = jnp.concatenate(
        [sizes, jnp.stack([lax.axis_index("sub"), lax.axis_index("cluster")]).astype(jnp.int32)]
    )
    map_row, map_column = slot_map[None, :], slot_map[:, None]
    halo = (half, lanes)
    vector = (order, columns)

    even, odd, even_cluster, odd_cluster = call(
        start_kernel, "start", [(half + mode_rows, lanes)] * 2 + [halo] * 2, [], info, rhs, basis
    )
    received = (
        pairs(even, "sub", 0),
        pairs(odd, "sub", 1),
        pairs(even_cluster, "cluster", 0),
        pairs(odd_cluster, "cluster", 1),
    )
    v0, near, packets = call(
        first_kernel, "first", [vector, (3 * modes, 2 * face), (modes, 4 * columns)], [], info, rhs, basis, *received
    )
    for step in steps("sub", 1):
        packets = jnp.concatenate([packets, swap(packets, "sub", step)], axis=0)

    work = pltpu.VMEM((order, 4 * columns), BF16)
    sends = [(half + moment_rows, lanes), halo, halo, halo]
    r0, y1, even, odd, even_cluster, odd_cluster, rows, gram01 = call(
        second_kernel,
        "second",
        [vector, vector] + sends + [(6 * modes, total), (columns, lanes)],
        [
            pltpu.VMEM((total, 4 * columns), F32),
            pltpu.VMEM((total + 2 * modes, total), F32),
            pltpu.VMEM((total, total), F32),
            work,
        ],
        info, packets, coarse, near, v0, map_row, map_column, operator,
    )
    received = (
        pairs(even, "sub", 0),
        pairs(odd, "sub", 1),
        pairs(even_cluster, "cluster", 0),
        pairs(odd_cluster, "cluster", 1),
    )
    moments = jnp.concatenate([even[half:], received[0][half:]], axis=0)
    for step in steps("sub", 2):
        moments = jnp.concatenate([moments, swap(moments, "sub", step)], axis=0)
    sums = [pltpu.VMEM((total + 2 * modes, columns), F32), pltpu.VMEM(vector, F32)]
    h1, y2, even, odd, even_cluster, odd_cluster, gram23 = call(
        third_kernel,
        "third",
        [vector, vector] + sends + [(columns, lanes)],
        sums + [work],
        info, y1, *received, moments, rows, near, map_row, map_column, operator,
    )
    grams = jnp.concatenate([gram01, gram23], axis=0)
    got_cluster = pairs(jnp.concatenate([even_cluster, grams], axis=0), "cluster", 0)
    grams = grams + got_cluster[half:]
    for step in steps("cluster", 2):
        grams = grams + swap(grams, "cluster", step)
    got = pairs(jnp.concatenate([even, grams], axis=0), "sub", 0)
    received = (got, pairs(odd, "sub", 1), got_cluster, pairs(odd_cluster, "cluster", 1))
    moments = jnp.concatenate([even[half:], got[half : half + moment_rows]], axis=0)
    grams = grams + got[half + moment_rows :]
    for step in steps("sub", 2):
        got = swap(jnp.concatenate([moments, grams], axis=0), "sub", step)
        grams = grams + got[moments.shape[0] :]
        moments = jnp.concatenate([moments, got[: moments.shape[0]]], axis=0)
    answer, rest = call(
        last_kernel, "last", [vector, vector], sums, info, y2, *received, moments, rows, near, r0, h1, grams
    )
    return answer[None, None], rest[None, None]


def solution(mesh):
    return jax.shard_map(
        shards,
        mesh=mesh,
        in_specs=(
            P("cluster", "sub", None, None),
            P("cluster", "sub", None, None),
            P("cluster", "sub", None),
            P("cluster", "sub", None),
            P("cluster", "sub", None, None),
            P("cluster", None, None),
        ),
        out_specs=(P("cluster", "sub", None, None), P("cluster", "sub", None, None)),
        check_vma=False,
    )
```

```python
import functools

import jax
import jax.numpy as jnp
from jax import lax
from jax.experimental import pallas as pl
from jax.experimental.pallas import tpu as pltpu
from jax.sharding import PartitionSpec as P

F32 = jnp.float32
BF16 = jnp.bfloat16


def matmul(left, right):
    return jnp.dot(left, right, precision=lax.Precision.HIGHEST, preferred_element_type=F32)


def passes(left, right):
    return jnp.dot(left, right, preferred_element_type=F32)


def pack(rows):
    half = rows.shape[0] // 2
    return jnp.concatenate([rows[:half], rows[half:]], axis=1)


def unpack(packed):
    half = packed.shape[1] // 2
    return jnp.concatenate([packed[:, :half], packed[:, half:]], axis=0)


def wide(values):
    first = values.astype(BF16).astype(F32)
    rest = values - first
    second = rest.astype(BF16).astype(F32)
    third = rest - second
    return jnp.concatenate(
        [
            jnp.concatenate([first, second], axis=1).astype(BF16),
            jnp.concatenate([third, jnp.zeros_like(third)], axis=1).astype(BF16),
        ],
        axis=1,
    )


def narrow(values):
    half = values.shape[1] // 2
    values = values[:, :half] + values[:, half:]
    half = half // 2
    return values[:, :half] + values[:, half:]


def operate(u, take, put, high, low, work_u, work_y, y_ref, face):
    order = high.shape[0]
    blocks = [slice(begin, begin + face) for begin in range(0, order, face)]
    parts = wide(u)
    for rows in blocks:
        work_u[rows, :] = passes(take[rows, :], parts).astype(BF16)
    parts = work_u[...]
    for rows in blocks:
        work_y[rows, :] = wide(narrow(passes(high[rows, :], parts) + passes(low[rows, :], parts)))
    parts = work_y[...]
    for rows in blocks:
        y_ref[rows, :] = narrow(passes(put[rows, :], parts))
    return gram(work_u[...], work_y[...])


def gram(left, right):
    full = lax.dot_general(left, right, (((0,), (0,)), ((), ())), preferred_element_type=F32)
    rows = full.shape[0] // 4
    full = (full[:rows] + full[rows : 2 * rows]) + full[2 * rows : 3 * rows]
    return narrow(full)


def grid(order):
    return (
        lax.broadcasted_iota(jnp.int32, (order, order), 0),
        lax.broadcasted_iota(jnp.int32, (order, order), 1),
    )


def write_symmetric(first, second, out):
    order = first.shape[0]
    row, column = grid(order)
    half = order // 2
    out[:half, :] = pack(jnp.where(row <= column, first, second))
    diagonal = jnp.sum(jnp.where(row == column, second, 0.0), axis=0, keepdims=True)
    out[half:, :order] = jnp.broadcast_to(diagonal, (out.shape[0] - half, order))
    out[half:, order:] = jnp.zeros((out.shape[0] - half, order), F32)


def read_symmetric(packed):
    order = packed.shape[1] // 2
    row, column = grid(order)
    both = unpack(packed[: order // 2, :])
    flipped = both.T
    diagonal = packed[order // 2 : order // 2 + 1, :order]
    first = jnp.where(row <= column, both, flipped)
    second = jnp.where(row < column, flipped, jnp.where(row == column, diagonal, both))
    return first, second


def parities(info):
    return info[4] % 2, info[5] % 2


def write_faces(info, source, outs, face):
    sub_odd, cluster_odd = parities(info)
    sides = (1 - sub_odd, sub_odd, 3 - cluster_odd, 2 + cluster_odd)
    for side, out in zip(sides, outs):
        out[: face // 2, :] = pack(source[pl.ds(pl.multiple_of(side * face, 16), face), :])


def facing_pair(odd, even_pair, odd_pair):
    return jnp.where(odd == 0, odd_pair, even_pair), jnp.where(odd == 0, even_pair, odd_pair)


def jump(info, source, packets, v_ref, face):
    sub_odd, cluster_odd = parities(info)
    half = face // 2
    halos = [packet[:half, :] for packet in packets]
    facing = facing_pair(sub_odd, halos[0], halos[1]) + facing_pair(cluster_odd, halos[2], halos[3])
    place = lax.broadcasted_iota(jnp.int32, (face, source.shape[1]), 0)
    for side in range(4):
        rows = slice(side * face, (side + 1) * face)
        v_ref[rows, :] = jnp.where(place < info[side], source[rows, :] - unpack(facing[side]), 0.0)


def start_kernel(info, rhs_t, basis, rhs_ref, even_ref, odd_ref, even_cluster_ref, odd_cluster_ref):
    face = rhs_t.shape[1] // 4
    modes = basis.shape[0]
    rhs_ref[...] = rhs_t[...].T
    write_faces(info, rhs_ref, (even_ref, odd_ref, even_cluster_ref, odd_cluster_ref), face)
    sub_odd, _ = parities(info)
    lower, upper = basis[:, :face], basis[:, face:]
    half = face // 2
    for out, chosen in (
        (even_ref, jnp.where(sub_odd == 0, upper, lower)),
        (odd_ref, jnp.where(sub_odd == 0, lower, upper)),
    ):
        lanes = out.shape[1]
        for i, begin in enumerate(range(0, face, lanes)):
            piece = chosen[:, begin : min(begin + lanes, face)]
            if piece.shape[1] < lanes:
                piece = jnp.concatenate([piece, jnp.zeros((modes, lanes - piece.shape[1]), F32)], axis=1)
            out[half + i * modes : half + (i + 1) * modes, :] = piece


def prepare_kernel(map_row, operator, take_ref, put_ref, high_ref, low_ref, buffer, arrived):
    order = operator.shape[0]
    face = order // 4
    blocks = [slice(begin, begin + face) for begin in range(0, order, face)]
    copies = [
        pltpu.make_async_copy(operator.at[pl.ds(rows.start, face)], buffer.at[pl.ds(rows.start, face)], arrived.at[i])
        for i, rows in enumerate(blocks)
    ]
    for copy in copies:
        copy.start()
    row = map_row[...]
    lanes = 128
    column = jnp.broadcast_to(row.astype(F32), (lanes, order)).T.astype(jnp.int32)
    lane = lax.broadcasted_iota(jnp.int32, (face, lanes), 1)
    line = lax.broadcasted_iota(jnp.int32, (face, order), 0)
    for rows in blocks:
        for begin in range(0, order, lanes):
            take_ref[rows, begin : begin + lanes] = (column[rows] == lane + begin).astype(F32).astype(BF16)
        put_ref[rows, :] = (row == line + rows.start).astype(F32).astype(BF16)
    for copy, rows in zip(copies, blocks):
        copy.wait()
        block = buffer[rows, :]
        high = block.astype(BF16)
        high_ref[rows, :] = high
        low_ref[rows, :] = (block - high.astype(F32)).astype(BF16)


def first_kernel(info, rhs, basis, even, odd, even_cluster, odd_cluster, v_ref, near_ref, lift_ref, packet_ref):
    face = rhs.shape[0] // 4
    modes = basis.shape[0]
    half = face // 2
    jump(info, rhs, (even, odd, even_cluster, odd_cluster), v_ref, face)
    sub_odd, _ = parities(info)

    def face_modes(packet):
        pieces = [packet[half + i : half + i + modes, :] for i in range(0, packet.shape[0] - half, modes)]
        return jnp.concatenate(pieces, axis=1)[:, :face]

    left, right = facing_pair(sub_odd, face_modes(even), face_modes(odd))
    zero = jnp.zeros_like(left)
    near = jnp.concatenate(
        [
            jnp.concatenate([-left, zero], axis=1),
            basis[...],
            jnp.concatenate([zero, -right], axis=1),
        ],
        axis=0,
    )
    place = lax.broadcasted_iota(jnp.int32, near.shape, 1)
    alive = jnp.logical_or(
        place < info[0], jnp.logical_and(place >= face, place < face + info[1])
    )
    near = jnp.where(alive, near, 0.0)
    near_ref[...] = near
    lift_ref[...] = near.T
    own = near[modes : 2 * modes]
    packet_ref[...] = jnp.zeros_like(packet_ref)
    packet_ref[: modes // 2, :] = pack(matmul(own, v_ref[: 2 * face, :]))
    packet_ref[modes // 2 :, : 3 * modes] = matmul(own, lift_ref[...])


def corrections(lift, rows, moments, modes):
    both = matmul(rows, moments)
    return matmul(lift[...], jnp.concatenate([both[: 3 * modes], both[3 * modes :]], axis=1))


def second_kernel(
    offsets, info, packets, coarse, near, lift, v0, take, put, high, low,
    r_ref, y_ref, even_ref, odd_ref, even_cluster_ref, odd_cluster_ref, rows_ref, packet_ref,
    moments, blocks, padded, product, work_u, work_y,
):
    order, columns = v0.shape
    face = order // 4
    modes = near.shape[0] // 3
    total = coarse.shape[0]
    me = info[4]
    for j, offset in enumerate(offsets):
        where = pl.ds(pl.multiple_of((me ^ offset) * modes, modes), modes)
        begin = j * (3 * modes // 2)
        moments[where, :] = unpack(packets[begin : begin + modes // 2, :])
        blocks[where, :] = packets[begin + modes // 2 : begin + 3 * modes // 2, :]
    padded[:modes, :] = jnp.zeros((modes, total), F32)
    padded[modes + total :, :] = jnp.zeros((modes, total), F32)
    padded[modes : modes + total, :] = coarse[...]
    for j in range(total // modes):
        rows = slice(j * modes, (j + 1) * modes)
        product[rows, :] = matmul(blocks[rows, : 3 * modes], padded[j * modes : (j + 3) * modes, :])
    once = padded[pl.ds(pl.multiple_of(me * modes, modes), 3 * modes), :]
    rows_ref[: 3 * modes, :] = once
    rows_ref[3 * modes :, :] = 2.0 * once - matmul(once, product[...])
    both = corrections(lift, rows_ref[...], moments[...], modes)
    r_ref[...] = v0[...]
    r_ref[: 2 * face, :] = v0[: 2 * face, :] - both[:, :columns]
    u = jnp.concatenate([v0[: 2 * face, :] - both[:, columns:], v0[2 * face :, :]], axis=0)
    curvature = operate(u, take, put, high, low, work_u, work_y, y_ref, face)
    write_faces(info, y_ref, (even_ref, odd_ref, even_cluster_ref, odd_cluster_ref), face)
    count = 3 * modes // 2
    packet_ref[:count, :] = pack(matmul(near[...], y_ref[: 2 * face, :]))
    r = wide(r_ref[...])
    write_symmetric(0.5 * gram(r, r), curvature, packet_ref.at[count:, :])


def third_kernel(
    offsets, info, y1, even, odd, even_cluster, odd_cluster, parts, rows, lift, take, put, high, low,
    h_ref, y_ref, even_ref, odd_ref, even_cluster_ref, odd_cluster_ref, gram_ref,
    moments, v_ref, work_u, work_y,
):
    order, columns = y1.shape
    face = order // 4
    modes = rows.shape[0] // 6
    count = 3 * modes // 2
    moments[...] = jnp.zeros_like(moments)
    for j, offset in enumerate(offsets):
        where = pl.ds(pl.multiple_of((info[4] ^ offset) * modes, modes), 3 * modes)
        moments[where, :] = moments[where, :] + unpack(parts[j * count : (j + 1) * count, :])
    jump(info, y1, (even, odd, even_cluster, odd_cluster), v_ref, face)
    both = corrections(lift, rows[...], moments[modes : moments.shape[0] - modes, :], modes)
    h_ref[...] = v_ref[...]
    h_ref[: 2 * face, :] = v_ref[: 2 * face, :] - both[:, :columns]
    u = jnp.concatenate([v_ref[: 2 * face, :] - both[:, columns:], v_ref[2 * face :, :]], axis=0)
    curvature = operate(u, take, put, high, low, work_u, work_y, y_ref, face)
    write_faces(info, y_ref, (even_ref, odd_ref, even_cluster_ref, odd_cluster_ref), face)
    h = wide(h_ref[...])
    write_symmetric(0.5 * gram(h, h), curvature, gram_ref)


def fourth_kernel(info, y2, near, even, odd, v_ref, packet_ref):
    face = y2.shape[0] // 4
    modes = near.shape[0] // 3
    sub_odd, _ = parities(info)
    half = face // 2
    place = lax.broadcasted_iota(jnp.int32, (face, y2.shape[1]), 0)
    for side, facing in enumerate(facing_pair(sub_odd, even[:half, :], odd[:half, :])):
        rows = slice(side * face, (side + 1) * face)
        v_ref[rows, :] = jnp.where(place < info[side], y2[rows, :] - unpack(facing), 0.0)
    packet_ref[...] = pack(matmul(near[modes : 2 * modes, :], v_ref[...]))


def spd_solve(matrix, target):
    order = matrix.shape[0]
    table = jnp.concatenate([matrix, target], axis=1)
    width = table.shape[1]
    size = 8
    lines = lax.broadcasted_iota(jnp.int32, (size, width), 0)
    rows = [table[i : i + size] for i in range(0, order, size)]
    for k in range(0, order, size):
        panel = rows[k // size]
        columns = [jnp.broadcast_to(panel[:, k + j : k + j + 1], (size, width)) for j in range(size)]
        for j in range(size):
            column = columns[j]
            inverse = 1.0 / column[j : j + 1]

            def eliminate(values):
                pivot = values[j : j + 1] * inverse
                return jnp.where(lines == j, pivot, values - column * pivot)

            panel = eliminate(panel)
            columns[j + 1 :] = [eliminate(other) for other in columns[j + 1 :]]
        for i in range(order // size):
            if i == k // size:
                continue
            values = rows[i]
            terms = [
                jnp.broadcast_to(values[:, k + j : k + j + 1], (size, width)) * panel[j : j + 1] for j in range(size)
            ]
            while len(terms) > 1:
                terms = [terms[t] + terms[t + 1] for t in range(0, len(terms), 2)]
            rows[i] = values - terms[0]
        rows[k // size] = panel
    return jnp.concatenate(rows, axis=0)[:, order:]


def step_kernel(grams, inverse_ref, step_ref):
    descent, curvature = read_symmetric(grams[...])
    order = curvature.shape[0]
    row, column = grid(order)
    inverse = spd_solve(curvature, jnp.where(row == column, 1.0, 0.0))
    inverse_ref[...] = inverse
    step_ref[:order, :] = matmul(inverse, descent)
    step_ref[order:, :] = curvature


def last_kernel(
    offsets, info, y2, upper, even_cluster, odd_cluster, parts, rows, lift, r0, h1, grams, inverse, step,
    solution_ref, residual_ref,
    moments, basis,
):
    order, columns = y2.shape
    face = order // 4
    modes = rows.shape[0] // 6
    half = face // 2
    for j, offset in enumerate(offsets):
        where = pl.ds(pl.multiple_of((info[4] ^ offset) * modes, modes), modes)
        moments[where, :] = unpack(parts[j * (modes // 2) : (j + 1) * (modes // 2), :])
    own = matmul(lift[...], matmul(rows[: 3 * modes, :], moments[...]))
    _, cluster_odd = parities(info)
    place = lax.broadcasted_iota(jnp.int32, (face, columns), 0)
    basis[:, :columns] = r0[...]
    basis[:, columns : 2 * columns] = h1[...]
    basis[: 2 * face, 2 * columns : 3 * columns] = upper[...] - own
    for i, facing in enumerate(facing_pair(cluster_odd, even_cluster[:half, :], odd_cluster[:half, :])):
        lines = slice((2 + i) * face, (3 + i) * face)
        basis[lines, 2 * columns : 3 * columns] = jnp.where(place < info[2 + i], y2[lines, :] - unpack(facing), 0.0)
    g2, g3 = read_symmetric(grams[...])
    first, g1 = step[:columns, :], step[columns:, :]
    mix = matmul(inverse[...], g2)
    last = spd_solve(g3 - matmul(g2, mix), matmul(g2, first) - g1)
    alpha = first + matmul(mix, last)
    zero = jnp.zeros_like(alpha)
    weights = jnp.concatenate(
        [
            jnp.concatenate([alpha, zero], axis=1),
            jnp.concatenate([-last, -alpha], axis=1),
            jnp.concatenate([zero, last], axis=1),
        ],
        axis=0,
    )
    both = matmul(basis[:, : 3 * columns], weights)
    both = both + jnp.concatenate([jnp.zeros_like(r0), r0[...]], axis=1)
    side = lax.broadcasted_iota(jnp.int32, (2 * columns, order), 1) // face
    both = jnp.where(side % 2 == 0, -both.T, both.T)
    solution_ref[...] = both[:columns]
    residual_ref[...] = both[columns:]


def call(kernel, name, outs, scratch, limit, *args, spaces=None):
    smem = pl.BlockSpec(memory_space=pltpu.SMEM)
    vmem = pl.BlockSpec(memory_space=pltpu.VMEM)
    return pl.pallas_call(
        kernel,
        name=name,
        out_shape=[out if hasattr(out, "dtype") else jax.ShapeDtypeStruct(out, F32) for out in outs],
        in_specs=spaces or [smem] + [vmem] * (len(args) - 1),
        out_specs=[vmem] * len(outs),
        scratch_shapes=scratch,
        compiler_params=pltpu.CompilerParams(vmem_limit_bytes=limit * 2**20),
    )(*args)


def pairs(value, axis, odd):
    peers = lax.axis_size(axis)
    low = [(i, i + 1) for i in range(odd, peers - 1, 2)]
    return lax.ppermute(value, axis, low + [(j, i) for i, j in low])


def swap(value, axis, step):
    return lax.ppermute(value, axis, [(i, i ^ step) for i in range(lax.axis_size(axis))])


def stages(axis, apart):
    bits = [1 << b for b in range(lax.axis_size(axis).bit_length() - 1)]
    tail = [[bits.pop(0)]] if apart else []
    groups = []
    while bits:
        group, bits = bits[:2], bits[2:]
        groups.insert(0, group + [sum(group)] if len(group) == 2 else group)
    return groups + tail


def spread(blocks, total, axis, apart):
    offsets = [0]
    for group in stages(axis, apart):
        pieces = [piece for piece in (blocks, total) if piece is not None]
        packet = jnp.concatenate(pieces, axis=0) if len(pieces) > 1 else pieces[0]
        got = [swap(packet, axis, step) for step in group]
        if total is not None:
            begin = 0 if blocks is None else blocks.shape[0]
            sums = [piece[begin:] for piece in got]
            total = total + sums[0] if len(sums) == 1 else (total + sums[0]) + (sums[1] + sums[2])
        if blocks is not None:
            count = blocks.shape[0]
            blocks = jnp.concatenate([blocks] + [piece[:count] for piece in got], axis=0)
        offsets = [offset ^ step for step in [0] + group for offset in offsets]
    return blocks, offsets, total


def shards(dual_ops, contributions, block_sizes, mult_map, coarse_basis, coarse_inverse):
    operator, rhs, sizes, slot_map = dual_ops[0, 0], contributions[0, 0], block_sizes[0, 0], mult_map[0, 0]
    basis, coarse = coarse_basis[0, 0], coarse_inverse[0]
    order, columns = rhs.shape
    face = order // 4
    half = face // 2
    modes = basis.shape[0]
    total = coarse.shape[0]
    lanes = 2 * columns
    mode_rows = -(-face // lanes) * modes
    gram_rows = columns // 2 + 8
    info = jnp.concatenate(
        [sizes, jnp.stack([lax.axis_index("sub"), lax.axis_index("cluster")]).astype(jnp.int32)]
    )
    halo = (half, lanes)
    vector = (order, columns)
    square = jax.ShapeDtypeStruct((order, order), BF16)

    rhs, even, odd, even_cluster, odd_cluster = call(
        start_kernel, "start", [vector] + [(half + mode_rows, lanes)] * 2 + [halo] * 2, [], 16, info, rhs.T, basis
    )
    vmem = pl.BlockSpec(memory_space=pltpu.VMEM)
    prepared = call(
        prepare_kernel,
        "prepare",
        [square] * 4,
        [pltpu.VMEM((order, order), F32), pltpu.SemaphoreType.DMA((4,))],
        32,
        slot_map[None, :], operator,
        spaces=[vmem, pl.BlockSpec(memory_space=pl.ANY)],
    )
    received = (
        pairs(even, "sub", 0),
        pairs(odd, "sub", 1),
        pairs(even_cluster, "cluster", 0),
        pairs(odd_cluster, "cluster", 1),
    )
    v0, near, lift, packet = call(
        first_kernel,
        "first",
        [vector, (3 * modes, 2 * face), (2 * face, 3 * modes), (3 * modes // 2, lanes)],
        [],
        16,
        info, rhs, basis, *received,
    )
    packets, offsets, _ = spread(packet, None, "sub", True)

    works = [pltpu.VMEM((order, 4 * columns), BF16)] * 2
    count = 3 * modes // 2
    r0, y1, even, odd, even_cluster, odd_cluster, rows, packet = call(
        functools.partial(second_kernel, offsets),
        "second",
        [vector, vector, halo, halo, halo, halo, (6 * modes, total), (count + gram_rows, lanes)],
        [
            pltpu.VMEM((total, columns), F32),
            pltpu.VMEM((total, lanes), F32),
            pltpu.VMEM((total + 2 * modes, total), F32),
            pltpu.VMEM((total, total), F32),
        ]
        + works,
        24,
        info, packets, coarse, near, lift, v0, *prepared,
    )
    parts, offsets, gram01 = spread(packet[:count], packet[count:], "sub", True)
    received = (
        pairs(even, "sub", 0),
        pairs(odd, "sub", 1),
        pairs(even_cluster, "cluster", 0),
        pairs(odd_cluster, "cluster", 1),
    )
    h1, y2, even, odd, even_cluster, odd_cluster, gram23 = call(
        functools.partial(third_kernel, offsets),
        "third",
        [vector, vector, halo, halo, halo, halo, (gram_rows, lanes)],
        [pltpu.VMEM((total + 2 * modes, columns), F32), pltpu.VMEM(vector, F32)] + works,
        24,
        info, y1, *received, parts, rows, lift, *prepared,
    )
    _, _, grams = spread(None, jnp.concatenate([gram01, gram23], axis=0), "cluster", False)
    even, odd = pairs(even, "sub", 0), pairs(odd, "sub", 1)
    upper, packet = call(
        fourth_kernel, "fourth", [(2 * face, columns), (modes // 2, lanes)], [], 16, info, y2, near, even, odd
    )
    inverse, step = call(
        step_kernel, "step", [(columns, columns), (2 * columns, columns)], [], 16, grams[:gram_rows], spaces=[vmem]
    )
    parts, offsets, gram23 = spread(packet, grams[gram_rows:], "sub", True)
    answer, rest = call(
        functools.partial(last_kernel, offsets),
        "last",
        [(columns, order)] * 2,
        [pltpu.VMEM((total, columns), F32), pltpu.VMEM((order, 4 * columns), F32)],
        16,
        info, y2, upper, pairs(even_cluster, "cluster", 0), pairs(odd_cluster, "cluster", 1),
        parts, rows, lift, r0, h1, gram23, inverse, step,
    )
    return answer.T[None, None], rest.T[None, None]


def solution(mesh):
    return jax.shard_map(
        shards,
        mesh=mesh,
        in_specs=(
            P("cluster", "sub", None, None),
            P("cluster", "sub", None, None),
            P("cluster", "sub", None),
            P("cluster", "sub", None),
            P("cluster", "sub", None, None),
            P("cluster", None, None),
        ),
        out_specs=(P("cluster", "sub", None, None), P("cluster", "sub", None, None)),
        check_vma=False,
    )
```

```python
import functools

import jax
import jax.numpy as jnp
from jax import lax
from jax.experimental import pallas as pl
from jax.experimental.pallas import tpu as pltpu
from jax.sharding import PartitionSpec as P

F32 = jnp.float32
BF16 = jnp.bfloat16


def matmul(left, right):
    return jnp.dot(left, right, precision=lax.Precision.HIGHEST, preferred_element_type=F32)


def passes(left, right):
    return jnp.dot(left, right, preferred_element_type=F32)


def halves(values):
    first = values.astype(BF16)
    return first, (values - first.astype(F32)).astype(BF16)


def quick(left, right):
    return fold(passes(jnp.concatenate(halves(left), axis=0), beside(right)))


def beside(right):
    first = right.astype(BF16).astype(F32)
    return jnp.concatenate([first, right - first], axis=1).astype(BF16)


def fold(products):
    rows, columns = products.shape[0] // 2, products.shape[1] // 2
    products = products[:rows] + products[rows:]
    return products[:, :columns] + products[:, columns:]


def pack(rows):
    half = rows.shape[0] // 2
    return jnp.concatenate([rows[:half], rows[half:]], axis=1)


def unpack(packed):
    half = packed.shape[1] // 2
    return jnp.concatenate([packed[:, :half], packed[:, half:]], axis=0)


def wide(values):
    first = values.astype(BF16).astype(F32)
    rest = values - first
    second = rest.astype(BF16).astype(F32)
    third = rest - second
    return jnp.concatenate(
        [
            jnp.concatenate([first, second], axis=1).astype(BF16),
            jnp.concatenate([third, jnp.zeros_like(third)], axis=1).astype(BF16),
        ],
        axis=1,
    )


def narrow(values):
    half = values.shape[1] // 2
    values = values[:, :half] + values[:, half:]
    half = half // 2
    return values[:, :half] + values[:, half:]


def operate(u, take, put, high, low, work_u, work_y, work, y_ref, face):
    order = take.shape[0]
    blocks = [slice(begin, begin + face) for begin in range(0, order, face)]
    parts = wide(u)
    for rows in blocks:
        work_u[rows, :] = passes(take[rows, :], parts).astype(BF16)
    parts = work_u[...]
    for rows in blocks:
        work_y[rows, :] = wide(narrow(passes(high[rows, :], parts) + passes(low[rows, :], parts)))
    parts = work_y[...]
    for rows in blocks:
        placed = passes(put[rows, :], parts)
        y_ref[rows, :] = narrow(placed)
        if rows.stop <= work.shape[0]:
            work[rows, :] = placed.astype(BF16)
    return gram(work_u[...], work_y[...])


def gram(left, right):
    full = lax.dot_general(left, right, (((0,), (0,)), ((), ())), preferred_element_type=F32)
    rows = full.shape[0] // 4
    full = (full[:rows] + full[rows : 2 * rows]) + full[2 * rows : 3 * rows]
    return narrow(full)


def grid(order):
    return (
        lax.broadcasted_iota(jnp.int32, (order, order), 0),
        lax.broadcasted_iota(jnp.int32, (order, order), 1),
    )


def write_symmetric(first, second, out):
    order = first.shape[0]
    row, column = grid(order)
    half = order // 2
    out[:half, :] = pack(jnp.where(row <= column, first, second))
    diagonal = jnp.sum(jnp.where(row == column, second, 0.0), axis=0, keepdims=True)
    out[half:, :order] = jnp.broadcast_to(diagonal, (out.shape[0] - half, order))
    out[half:, order:] = jnp.zeros((out.shape[0] - half, order), F32)


def read_symmetric(packed):
    order = packed.shape[1] // 2
    row, column = grid(order)
    both = unpack(packed[: order // 2, :])
    flipped = both.T
    diagonal = packed[order // 2 : order // 2 + 1, :order]
    first = jnp.where(row <= column, both, flipped)
    second = jnp.where(row < column, flipped, jnp.where(row == column, diagonal, both))
    return first, second


def parities(position):
    return position[0] % 2, position[1] % 2


def write_faces(position, source, outs, face):
    sub_odd, cluster_odd = parities(position)
    sides = (1 - sub_odd, sub_odd, 3 - cluster_odd, 2 + cluster_odd)
    for side, out in zip(sides, outs):
        out[: face // 2, :] = pack(source[pl.ds(pl.multiple_of(side * face, 16), face), :])


def facing_pair(odd, even_pair, odd_pair):
    return jnp.where(odd == 0, odd_pair, even_pair), jnp.where(odd == 0, even_pair, odd_pair)


def jump(position, source, packets, v_ref, face):
    sub_odd, cluster_odd = parities(position)
    half = face // 2
    halos = [packet[:half, :] for packet in packets]
    facing = facing_pair(sub_odd, halos[0], halos[1]) + facing_pair(cluster_odd, halos[2], halos[3])
    place = lax.broadcasted_iota(jnp.int32, (face, source.shape[1]), 0)
    for side in range(4):
        rows = slice(side * face, (side + 1) * face)
        v_ref[rows, :] = jnp.where(place < position[2 + side], source[rows, :] - unpack(facing[side]), 0.0)


def start_kernel(
    position, rhs_t, basis, map_row, rhs_ref, basis_ref, map_ref, even_ref, odd_ref, even_cluster_ref, odd_cluster_ref, buffer, arrived
):
    copies = [
        pltpu.make_async_copy(rhs_t, buffer, arrived.at[0]),
        pltpu.make_async_copy(basis, basis_ref, arrived.at[1]),
        pltpu.make_async_copy(map_row, map_ref, arrived.at[2]),
    ]
    for copy in copies:
        copy.start()
    face = rhs_t.shape[1] // 4
    modes = basis.shape[0]
    copies[0].wait()
    rhs_ref[...] = buffer[...].T
    write_faces(position, rhs_ref, (even_ref, odd_ref, even_cluster_ref, odd_cluster_ref), face)
    copies[1].wait()
    copies[2].wait()
    sub_odd, _ = parities(position)
    lower, upper = basis_ref[:, :face], basis_ref[:, face:]
    half = face // 2
    for out, chosen in (
        (even_ref, jnp.where(sub_odd == 0, upper, lower)),
        (odd_ref, jnp.where(sub_odd == 0, lower, upper)),
    ):
        lanes = out.shape[1]
        for i, begin in enumerate(range(0, face, lanes)):
            piece = chosen[:, begin : min(begin + lanes, face)]
            if piece.shape[1] < lanes:
                piece = jnp.concatenate([piece, jnp.zeros((modes, lanes - piece.shape[1]), F32)], axis=1)
            out[half + i * modes : half + (i + 1) * modes, :] = piece


def permutation_kernel(map_row, take_ref, put_ref):
    order = map_row.shape[1]
    face = order // 4
    row = map_row[...]
    lanes = 128
    column = jnp.broadcast_to(row.astype(F32), (lanes, order)).T.astype(jnp.int32)
    lane = lax.broadcasted_iota(jnp.int32, (face, lanes), 1)
    line = lax.broadcasted_iota(jnp.int32, (face, order), 0)
    for first in range(0, order, face):
        rows = slice(first, first + face)
        for begin in range(0, order, lanes):
            take_ref[rows, begin : begin + lanes] = (column[rows] == lane + begin).astype(F32).astype(BF16)
        put_ref[rows, :] = (row == line + first).astype(F32).astype(BF16)


def operator_kernel(operator, high_ref, low_ref, buffer, arrived):
    size = buffer.shape[0] // arrived.shape[0]
    copies = [
        pltpu.make_async_copy(
            operator.at[pl.ds(i * size, size)], buffer.at[pl.ds(i * size, size)], arrived.at[i]
        )
        for i in range(arrived.shape[0])
    ]
    for copy in copies:
        copy.start()
    for i, copy in enumerate(copies):
        copy.wait()
        rows = slice(i * size, (i + 1) * size)
        block = buffer[rows, :]
        high = block.astype(BF16)
        high_ref[rows, :] = high
        low_ref[rows, :] = (block - high.astype(F32)).astype(BF16)


def first_kernel(position, rhs, basis, even, odd, even_cluster, odd_cluster, v_ref, near_ref, near_parts_ref, lift_ref, packet_ref):
    face = rhs.shape[0] // 4
    modes = basis.shape[0]
    half = face // 2
    jump(position, rhs, (even, odd, even_cluster, odd_cluster), v_ref, face)
    sub_odd, _ = parities(position)

    def face_modes(packet):
        pieces = [packet[half + i : half + i + modes, :] for i in range(0, packet.shape[0] - half, modes)]
        return jnp.concatenate(pieces, axis=1)[:, :face]

    left, right = facing_pair(sub_odd, face_modes(even), face_modes(odd))
    zero = jnp.zeros_like(left)
    near = jnp.concatenate(
        [
            jnp.concatenate([-left, zero], axis=1),
            basis[...],
            jnp.concatenate([zero, -right], axis=1),
        ],
        axis=0,
    )
    place = lax.broadcasted_iota(jnp.int32, near.shape, 1)
    alive = jnp.logical_or(
        place < position[2], jnp.logical_and(place >= face, place < face + position[3])
    )
    near = jnp.where(alive, near, 0.0)
    near_ref[...] = near
    across = near.T
    near_parts_ref[...] = jnp.concatenate(halves(near), axis=0)
    lift_ref[...] = beside(across)
    own = near[modes : 2 * modes]
    packet_ref[...] = jnp.zeros_like(packet_ref)
    packet_ref[: modes // 2, :] = pack(matmul(own, v_ref[: 2 * face, :]))
    packet_ref[modes // 2 :, : 3 * modes] = matmul(own, across)


def lift_both(lift, once, twice):
    both = jnp.concatenate([once, twice], axis=1)
    first = both.astype(BF16).astype(F32)
    factor = jnp.concatenate(
        [
            jnp.concatenate([first, both - first], axis=1),
            jnp.concatenate([first, jnp.zeros_like(first)], axis=1),
        ],
        axis=0,
    ).astype(BF16)
    return narrow_once(passes(lift[...], factor))


def narrow_once(values):
    half = values.shape[1] // 2
    return values[:, :half] + values[:, half:]


def advance(u, take, put, high, low, near_parts, squared, work_u, work_y, work, y_ref, packet_ref, face, count):
    curvature = operate(u, take, put, high, low, work_u, work_y, work, y_ref, face)
    moments = passes(near_parts[...], work[...])
    packet_ref[:count, :] = pack(narrow(moments[: 2 * count] + moments[2 * count :]))
    parts = wide(squared[...])
    write_symmetric(0.5 * gram(parts, parts), curvature, packet_ref.at[count:, :])


def place_coarse(coarse, padded, modes):
    total = coarse.shape[0]
    padded[:modes, :] = jnp.zeros((modes, total), F32)
    padded[modes + total :, :] = jnp.zeros((modes, total), F32)
    padded[modes : modes + total, :] = coarse[...]


def place_blocks(offsets, position, packets, blocks, modes):
    for j, offset in enumerate(offsets):
        where = pl.ds(pl.multiple_of((position[0] ^ offset) * modes, modes), modes)
        begin = j * (3 * modes // 2) + modes // 2
        blocks[where, :] = packets[begin : begin + modes, :]


def second_kernel(
    offsets, position, packets, coarse, near_parts, lift, v0, take, put, high, low,
    r_ref, y_ref, even_ref, odd_ref, even_cluster_ref, odd_cluster_ref, packet_ref,
    moments, blocks, padded, image, work_u, work_y, work,
):
    order, columns = v0.shape
    face = order // 4
    modes = near_parts.shape[0] // 6
    total = coarse.shape[0]
    me = position[0]
    for j, offset in enumerate(offsets):
        where = pl.ds(pl.multiple_of((me ^ offset) * modes, modes), modes)
        begin = j * (3 * modes // 2)
        moments[where, :] = unpack(packets[begin : begin + modes // 2, :])
    place_blocks(offsets, position, packets, blocks, modes)
    place_coarse(coarse, padded, modes)
    image[:modes, :] = jnp.zeros((modes, columns), F32)
    image[modes + total :, :] = jnp.zeros((modes, columns), F32)
    image[modes : modes + total, :] = quick(coarse[...], moments[...])
    own = pl.ds(pl.multiple_of(me * modes, modes), 3 * modes)
    near_rows = padded[own, :]
    again = [
        quick(blocks[j * modes : (j + 1) * modes, : 3 * modes], image[j * modes : (j + 3) * modes, :])
        for j in range(total // modes)
    ]
    once = image[own, :]
    both = lift_both(lift, once, 2.0 * once - quick(near_rows, jnp.concatenate(again, axis=0)))
    r_ref[...] = v0[...]
    r_ref[: 2 * face, :] = v0[: 2 * face, :] - both[:, :columns]
    u = jnp.concatenate([v0[: 2 * face, :] - both[:, columns:], v0[2 * face :, :]], axis=0)
    advance(u, take, put, high, low, near_parts, r_ref, work_u, work_y, work, y_ref, packet_ref, face, 3 * modes // 2)
    write_faces(position, y_ref, (even_ref, odd_ref, even_cluster_ref, odd_cluster_ref), face)


def rows_kernel(offsets, position, packets, coarse, rows_ref, blocks, padded, product, columns_ref):
    total = coarse.shape[0]
    count = rows_ref.shape[1] // (2 * len(offsets))
    modes = 2 * count // 3
    place_blocks(offsets, position, packets, blocks, modes)
    place_coarse(coarse, padded, modes)
    for j in range(total // modes):
        rows = slice(j * modes, (j + 1) * modes)
        product[rows, :] = matmul(blocks[rows, : 3 * modes], padded[j * modes : (j + 3) * modes, :])
    once = padded[pl.ds(pl.multiple_of(position[0] * modes, modes), 3 * modes), :]
    columns_ref[...] = jnp.zeros_like(columns_ref)
    columns_ref[modes : modes + total, : 3 * modes] = once.T
    columns_ref[modes : modes + total, 3 * modes :] = (2.0 * once - matmul(once, product[...])).T
    pieces = [
        columns_ref[pl.ds(pl.multiple_of((position[0] ^ offset) * modes + begin, 16), count), :]
        for begin in (0, count)
        for offset in offsets
    ]
    rows_ref[...] = jnp.concatenate(halves(jnp.concatenate(pieces, axis=0).T), axis=0)


def coefficients(rows, parts):
    half = parts.shape[1] // 2
    moments = jnp.concatenate([parts[:, :half], parts[:, half:]], axis=0)
    return fold(passes(rows[...], beside(moments)))


def third_kernel(
    position, y1, even, odd, even_cluster, odd_cluster, parts, rows, near_parts, lift, take, put, high, low,
    h_ref, y_ref, even_ref, odd_ref, even_cluster_ref, odd_cluster_ref, packet_ref,
    v_ref, work_u, work_y, work,
):
    order, columns = y1.shape
    face = order // 4
    modes = near_parts.shape[0] // 6
    jump(position, y1, (even, odd, even_cluster, odd_cluster), v_ref, face)
    both = coefficients(rows, parts)
    both = lift_both(lift, both[: 3 * modes], both[3 * modes :])
    h_ref[...] = v_ref[...]
    h_ref[: 2 * face, :] = v_ref[: 2 * face, :] - both[:, :columns]
    u = jnp.concatenate([v_ref[: 2 * face, :] - both[:, columns:], v_ref[2 * face :, :]], axis=0)
    advance(u, take, put, high, low, near_parts, h_ref, work_u, work_y, work, y_ref, packet_ref, face, 3 * modes // 2)
    write_faces(position, y_ref, (even_ref, odd_ref, even_cluster_ref, odd_cluster_ref), face)


def stack_kernel(position, y2, even, odd, even_cluster, odd_cluster, r0, h1, basis_ref, v_ref):
    face = y2.shape[0] // 4
    jump(position, y2, (even, odd, even_cluster, odd_cluster), v_ref, face)
    columns = y2.shape[1]
    basis_ref[: 2 * columns, :] = jnp.concatenate([r0[...], h1[...]], axis=1).T
    basis_ref[2 * columns :, :] = v_ref[...].T


def spd_solve(matrix, target):
    order = matrix.shape[0]
    table = jnp.concatenate([matrix, target], axis=1)
    width = table.shape[1]
    size = 8
    lines = lax.broadcasted_iota(jnp.int32, (size, width), 0)
    rows = [table[i : i + size] for i in range(0, order, size)]
    for k in range(0, order, size):
        panel = rows[k // size]
        columns = [jnp.broadcast_to(panel[:, k + j : k + j + 1], (size, width)) for j in range(size)]
        for j in range(size):
            column = columns[j]
            inverse = 1.0 / column[j : j + 1]

            def eliminate(values):
                pivot = values[j : j + 1] * inverse
                return jnp.where(lines == j, pivot, values - column * pivot)

            panel = eliminate(panel)
            columns[j + 1 :] = [eliminate(other) for other in columns[j + 1 :]]
        for i in range(order // size):
            if i == k // size:
                continue
            values = rows[i]
            terms = [
                jnp.broadcast_to(values[:, k + j : k + j + 1], (size, width)) * panel[j : j + 1] for j in range(size)
            ]
            while len(terms) > 1:
                terms = [terms[t] + terms[t + 1] for t in range(0, len(terms), 2)]
            rows[i] = values - terms[0]
        rows[k // size] = panel
    return jnp.concatenate(rows, axis=0)[:, order:]


def step_kernel(grams, inverse_ref, step_ref):
    descent, curvature = read_symmetric(grams[: grams.shape[0] // 2, :])
    order = curvature.shape[0]
    row, column = grid(order)
    inverse = spd_solve(curvature, jnp.where(row == column, 1.0, 0.0))
    inverse_ref[...] = inverse
    step_ref[:order, :] = matmul(inverse, descent)
    step_ref[order:, :] = curvature


def last_kernel(
    parts, rows, near, basis, grams, inverse, step,
    solution_ref, residual_ref,
):
    columns = basis.shape[0] // 3
    order = basis.shape[1]
    face = order // 4
    own = coefficients(rows, parts)[: near.shape[0]]
    g2, g3 = read_symmetric(grams[...])
    first, g1 = step[:columns, :], step[columns:, :]
    mix = matmul(inverse[...], g2)
    last = spd_solve(g3 - matmul(g2, mix), matmul(g2, first) - g1)
    alpha = first + matmul(mix, last)
    zero = jnp.zeros_like(alpha)
    weights = jnp.concatenate(
        [
            jnp.concatenate([alpha, zero], axis=1),
            jnp.concatenate([-last, -alpha], axis=1),
            jnp.concatenate([zero, last], axis=1),
        ],
        axis=0,
    )
    both = matmul(weights.T, basis[...])
    lifted = matmul(matmul(own, last).T, near[...])
    side = lax.broadcasted_iota(jnp.int32, (columns, order), 1) // face
    answer = both[:columns]
    rest = basis[:columns, :] + both[columns:] - jnp.concatenate([lifted, jnp.zeros_like(lifted)], axis=1)
    solution_ref[...] = jnp.where(side % 2 == 0, -answer, answer)
    residual_ref[...] = jnp.where(side % 2 == 0, -rest, rest)


SMEM = pl.BlockSpec(memory_space=pltpu.SMEM)
VMEM = pl.BlockSpec(memory_space=pltpu.VMEM)
HBM = pl.BlockSpec(memory_space=pltpu.HBM)


def in_hbm(value):
    return pltpu.with_memory_space_constraint(value, pltpu.HBM)


def call(kernel, name, outs, scratch, limit, *args, spaces=(), work=None):
    spaces = list(spaces)
    return pl.pallas_call(
        kernel,
        name=name,
        out_shape=[out if hasattr(out, "dtype") else jax.ShapeDtypeStruct(out, F32) for out in outs],
        in_specs=spaces + [VMEM] * (len(args) - len(spaces)),
        out_specs=[VMEM] * len(outs),
        scratch_shapes=scratch,
        cost_estimate=work and pl.CostEstimate(flops=0, transcendentals=0, bytes_accessed=work),
        compiler_params=pltpu.CompilerParams(vmem_limit_bytes=limit * 2**20),
    )(*args)


def pairs(value, axis, odd):
    peers = lax.axis_size(axis)
    low = [(i, i + 1) for i in range(odd, peers - 1, 2)]
    return lax.ppermute(value, axis, low + [(j, i) for i, j in low])


def swap(value, axis, step):
    return lax.ppermute(value, axis, [(i, i ^ step) for i in range(lax.axis_size(axis))])


def steps(axis):
    return [1 << b for b in reversed(range(lax.axis_size(axis).bit_length() - 1))]


def tie(value, others):
    return lax.optimization_barrier((value, *others))[0] if others else value


def join(blocks, total):
    pieces = [piece for piece in (blocks, total) if piece is not None]
    return jnp.concatenate(pieces, axis=0) if len(pieces) > 1 else pieces[0]


def exchange(blocks, total, axis, group, after=()):
    packet = tie(join(blocks, total), after)
    got = [swap(packet, axis, step) for step in group]
    count = 0 if blocks is None else blocks.shape[0]
    if blocks is not None:
        blocks = jnp.concatenate([blocks] + [piece[:count] for piece in got], axis=0)
    if total is not None:
        sums = [piece[count:] for piece in got]
        total = total + sums[0] if len(sums) == 1 else (total + sums[0]) + (sums[1] + sums[2])
    return blocks, total


def spread(blocks, total, axis, after):
    offsets = [0]
    far = steps(axis)[:-1]
    groups = [far[i : i + 2] for i in range(0, len(far), 2)]
    for group in groups + [[1]]:
        group = group + [sum(group)] if len(group) == 2 else group
        blocks, total = exchange(blocks, total, axis, group, after if group == [1] else ())
        offsets = [offset ^ step for step in [0] + group for offset in offsets]
    return blocks, total, offsets


def peer_offsets(axis):
    offsets = [0]
    for step in steps(axis):
        offsets = offsets + [offset ^ step for offset in offsets]
    return offsets


def halos(even, odd, even_cluster, odd_cluster):
    return (
        pairs(even, "sub", 0),
        pairs(odd, "sub", 1),
        pairs(even_cluster, "cluster", 0),
        pairs(odd_cluster, "cluster", 1),
    )


def shards(dual_ops, contributions, block_sizes, mult_map, coarse_basis, coarse_inverse):
    operator, rhs, sizes, slot_map = dual_ops[0, 0], contributions[0, 0], block_sizes[0, 0], mult_map[0, 0]
    basis, coarse = coarse_basis[0, 0], coarse_inverse[0]
    order, columns = rhs.shape
    face = order // 4
    half = face // 2
    modes = basis.shape[0]
    total = coarse.shape[0]
    lanes = 2 * columns
    mode_rows = -(-face // lanes) * modes
    gram_rows = columns // 2 + 8
    position = jnp.concatenate(
        [jnp.stack([lax.axis_index("sub"), lax.axis_index("cluster")]).astype(jnp.int32), sizes]
    )
    halo = (half, lanes)
    vector = (order, columns)
    square = jax.ShapeDtypeStruct((order, order), BF16)
    count = 3 * modes // 2

    map_row = slot_map[None, :]
    rhs, basis, map_row, *faces = call(
        start_kernel,
        "start",
        [vector, basis.shape, jax.ShapeDtypeStruct(map_row.shape, jnp.int32)] + [(half + mode_rows, lanes)] * 2 + [halo] * 2,
        [pltpu.VMEM((columns, order), F32), pltpu.SemaphoreType.DMA((3,))],
        16,
        position, in_hbm(rhs.T), in_hbm(basis), in_hbm(map_row),
        spaces=(SMEM, HBM, HBM, HBM),
    )
    permutations = call(permutation_kernel, "permutation", [square] * 2, [], 24, map_row, work=4 * 2**20)
    received = halos(*faces)
    v0, near, near_parts, lift, packet = call(
        first_kernel,
        "first",
        [
            vector,
            (3 * modes, 2 * face),
            jax.ShapeDtypeStruct((6 * modes, 2 * face), BF16),
            jax.ShapeDtypeStruct((2 * face, 6 * modes), BF16),
            (count, lanes),
        ],
        [],
        16,
        position, tie(rhs, permutations), basis, *received,
        spaces=(SMEM,),
    )
    operators = call(
        operator_kernel,
        "operator",
        [square] * 2,
        [pltpu.VMEM((order, order), F32), pltpu.SemaphoreType.DMA((8,))],
        32,
        in_hbm(tie(operator, (packet,))),
        spaces=(HBM,),
        work=8 * 2**20,
    )
    packets, _, offsets = spread(packet, None, "sub", operators)

    works = [pltpu.VMEM((rows, 4 * columns), BF16) for rows in (order, order, 2 * face)]
    padded = [pltpu.VMEM((total, lanes), F32), pltpu.VMEM((total + 2 * modes, total), F32)]
    sends = [halo] * 4 + [(count + gram_rows, lanes)]
    r0, y1, *faces, packet = call(
        functools.partial(second_kernel, offsets),
        "second",
        [vector, vector] + sends,
        [pltpu.VMEM((total, columns), F32)] + padded + [pltpu.VMEM((total + 2 * modes, columns), F32)] + works,
        24,
        position, packets, coarse, near_parts, lift, v0, *permutations, *operators,
        spaces=(SMEM,),
    )
    received = halos(*faces)
    parts, gram01, _ = spread(packet[:count], packet[count:], "sub", received)
    packets, *_ = lax.optimization_barrier((packets, *received))
    (rows,) = call(
        functools.partial(rows_kernel, offsets),
        "rows",
        [jax.ShapeDtypeStruct((12 * modes, 2 * parts.shape[0]), BF16)],
        padded + [pltpu.VMEM((total, total), F32), pltpu.VMEM((total + 2 * modes, 6 * modes), F32)],
        16,
        position, packets, coarse,
        spaces=(SMEM,),
        work=2 * 2**20,
    )
    h1, y2, *faces, packet = call(
        third_kernel,
        "third",
        [vector, vector] + sends,
        [pltpu.VMEM(vector, F32)] + works,
        24,
        position, y1, *received, parts, rows, near_parts, lift, *permutations, *operators,
        spaces=(SMEM,),
    )
    grams = jnp.concatenate([gram01, packet[count:]], axis=0)
    received = halos(*faces)
    for step in steps("cluster"):
        _, grams = exchange(None, grams, "cluster", [step], received[:2] if step == 1 else ())
    grams = tie(grams, received[2:])
    inverse, step0 = call(
        step_kernel, "step", [(columns, columns), (2 * columns, columns)], [], 16, grams, work=4 * 2**20
    )
    parts, gram23 = packet[:count], grams[gram_rows:]
    previous = ()
    stacked = None
    for step in steps("sub"):
        parts, gram23 = exchange(parts, gram23, "sub", [step], previous)
        if not previous:
            previous = (inverse,)
            (stacked,) = call(
                stack_kernel,
                "stack",
                [(3 * columns, order)],
                [pltpu.VMEM(vector, F32)],
                16,
                position, tie(y2, (gram23,)), *received, r0, h1,
                spaces=(SMEM,),
                work=4 * 2**20,
            )
        else:
            previous = (stacked,)
    answer, rest = call(
        last_kernel,
        "last",
        [(columns, order)] * 2,
        [],
        16,
        parts, rows, near, stacked, gram23, inverse, step0,
    )
    return answer.T[None, None], rest.T[None, None]


def solution(mesh):
    return jax.shard_map(
        shards,
        mesh=mesh,
        in_specs=(
            P("cluster", "sub", None, None),
            P("cluster", "sub", None, None),
            P("cluster", "sub", None),
            P("cluster", "sub", None),
            P("cluster", "sub", None, None),
            P("cluster", None, None),
        ),
        out_specs=(P("cluster", "sub", None, None), P("cluster", "sub", None, None)),
        check_vma=False,
    )
```

```python
import functools

import jax
import jax.numpy as jnp
from jax import lax
from jax.experimental import pallas as pl
from jax.experimental.pallas import tpu as pltpu
from jax.sharding import PartitionSpec as P

F32 = jnp.float32
BF16 = jnp.bfloat16


def matmul(left, right):
    return jnp.dot(left, right, precision=lax.Precision.HIGHEST, preferred_element_type=F32)


def matmul_nt(left, right):
    return lax.dot_general(
        left, right, (((1,), (1,)), ((), ())), precision=lax.Precision.HIGHEST, preferred_element_type=F32
    )


def passes(left, right):
    return jnp.dot(left, right, preferred_element_type=F32)


def halves(values):
    first = values.astype(BF16)
    return first, (values - first.astype(F32)).astype(BF16)


def quick(left, right):
    return fold(passes(jnp.concatenate(halves(left), axis=0), beside(right)))


def beside(right):
    first = right.astype(BF16).astype(F32)
    return jnp.concatenate([first, right - first], axis=1).astype(BF16)


def fold(products):
    rows, columns = products.shape[0] // 2, products.shape[1] // 2
    products = products[:rows] + products[rows:]
    return products[:, :columns] + products[:, columns:]


def pack(rows):
    half = rows.shape[0] // 2
    return jnp.concatenate([rows[:half], rows[half:]], axis=1)


def unpack(packed):
    half = packed.shape[1] // 2
    return jnp.concatenate([packed[:, :half], packed[:, half:]], axis=0)


def wide(values):
    first = values.astype(BF16).astype(F32)
    rest = values - first
    second = rest.astype(BF16).astype(F32)
    third = rest - second
    return jnp.concatenate(
        [
            jnp.concatenate([first, second], axis=1).astype(BF16),
            jnp.concatenate([third, jnp.zeros_like(third)], axis=1).astype(BF16),
        ],
        axis=1,
    )


def narrow(values):
    half = values.shape[1] // 2
    values = values[:, :half] + values[:, half:]
    half = half // 2
    return values[:, :half] + values[:, half:]


def operate(u, take, put, high, low, work_u, work_y, work, y_ref, face):
    order = take.shape[0]
    blocks = [slice(begin, begin + face) for begin in range(0, order, face)]
    parts = wide(u)
    for rows in blocks:
        work_u[rows, :] = passes(take[rows, :], parts).astype(BF16)
    parts = work_u[...]
    for rows in blocks:
        work_y[rows, :] = wide(narrow(passes(high[rows, :], parts) + passes(low[rows, :], parts)))
    parts = work_y[...]
    for rows in blocks:
        placed = passes(put[rows, :], parts)
        y_ref[rows, :] = narrow(placed)
        if rows.stop <= work.shape[0]:
            work[rows, :] = placed.astype(BF16)
    return gram(work_u[...], work_y[...])


def gram(left, right):
    full = lax.dot_general(left, right, (((0,), (0,)), ((), ())), preferred_element_type=F32)
    rows = full.shape[0] // 4
    full = (full[:rows] + full[rows : 2 * rows]) + full[2 * rows : 3 * rows]
    return narrow(full)


def grid(order):
    return (
        lax.broadcasted_iota(jnp.int32, (order, order), 0),
        lax.broadcasted_iota(jnp.int32, (order, order), 1),
    )


def write_symmetric(first, second, out):
    order = first.shape[0]
    row, column = grid(order)
    half = order // 2
    out[:half, :] = pack(jnp.where(row <= column, first, second))
    diagonal = jnp.sum(jnp.where(row == column, second, 0.0), axis=0, keepdims=True)
    out[half:, :order] = jnp.broadcast_to(diagonal, (out.shape[0] - half, order))
    out[half:, order:] = jnp.zeros((out.shape[0] - half, order), F32)


def read_symmetric(packed):
    order = packed.shape[1] // 2
    row, column = grid(order)
    both = unpack(packed[: order // 2, :])
    flipped = both.T
    diagonal = packed[order // 2 : order // 2 + 1, :order]
    first = jnp.where(row <= column, both, flipped)
    second = jnp.where(row < column, flipped, jnp.where(row == column, diagonal, both))
    return first, second


def parities(position):
    return position[0] % 2, position[1] % 2


def write_faces(position, source, outs, face):
    sub_odd, cluster_odd = parities(position)
    sides = (1 - sub_odd, sub_odd, 3 - cluster_odd, 2 + cluster_odd)
    for side, out in zip(sides, outs):
        out[: face // 2, :] = pack(source[pl.ds(pl.multiple_of(side * face, 16), face), :])


def facing_pair(odd, even_pair, odd_pair):
    return jnp.where(odd == 0, odd_pair, even_pair), jnp.where(odd == 0, even_pair, odd_pair)


def jump(position, source, packets, v_ref, face):
    sub_odd, cluster_odd = parities(position)
    half = face // 2
    halos = [packet[:half, :] for packet in packets]
    facing = facing_pair(sub_odd, halos[0], halos[1]) + facing_pair(cluster_odd, halos[2], halos[3])
    place = lax.broadcasted_iota(jnp.int32, (face, source.shape[1]), 0)
    for side in range(4):
        rows = slice(side * face, (side + 1) * face)
        v_ref[rows, :] = jnp.where(place < position[2 + side], source[rows, :] - unpack(facing[side]), 0.0)


def start_kernel(
    rhs_t, basis, map_row, rhs_ref, basis_ref, map_ref, even_ref, odd_ref, even_cluster_ref, odd_cluster_ref, buffer, arrived
):
    copies = [
        pltpu.make_async_copy(rhs_t, buffer, arrived.at[0]),
        pltpu.make_async_copy(basis, basis_ref, arrived.at[1]),
        pltpu.make_async_copy(map_row, map_ref, arrived.at[2]),
    ]
    for copy in copies:
        copy.start()
    face = rhs_t.shape[1] // 4
    modes = basis.shape[0]
    position = (lax.axis_index("sub"), lax.axis_index("cluster"))
    copies[0].wait()
    rhs_ref[...] = buffer[...].T
    write_faces(position, rhs_ref, (even_ref, odd_ref, even_cluster_ref, odd_cluster_ref), face)
    copies[1].wait()
    copies[2].wait()
    sub_odd, _ = parities(position)
    lower, upper = basis_ref[:, :face], basis_ref[:, face:]
    half = face // 2
    for out, chosen in (
        (even_ref, jnp.where(sub_odd == 0, upper, lower)),
        (odd_ref, jnp.where(sub_odd == 0, lower, upper)),
    ):
        lanes = out.shape[1]
        for i, begin in enumerate(range(0, face, lanes)):
            piece = chosen[:, begin : min(begin + lanes, face)]
            if piece.shape[1] < lanes:
                piece = jnp.concatenate([piece, jnp.zeros((modes, lanes - piece.shape[1]), F32)], axis=1)
            out[half + i * modes : half + (i + 1) * modes, :] = piece


def permutation_kernel(map_row, take_ref, put_ref):
    order = map_row.shape[1]
    face = order // 4
    row = map_row[...]
    lanes = 128
    column = jnp.broadcast_to(row.astype(F32), (lanes, order)).T.astype(jnp.int32)
    lane = lax.broadcasted_iota(jnp.int32, (face, lanes), 1)
    line = lax.broadcasted_iota(jnp.int32, (face, order), 0)
    for first in range(0, order, face):
        rows = slice(first, first + face)
        for begin in range(0, order, lanes):
            take_ref[rows, begin : begin + lanes] = (column[rows] == lane + begin).astype(F32).astype(BF16)
        put_ref[rows, :] = (row == line + first).astype(F32).astype(BF16)


def operator_kernel(operator, high_ref, low_ref, buffer, arrived):
    size = buffer.shape[0] // arrived.shape[0]
    copies = [
        pltpu.make_async_copy(
            operator.at[pl.ds(i * size, size)], buffer.at[pl.ds(i * size, size)], arrived.at[i]
        )
        for i in range(arrived.shape[0])
    ]
    for copy in copies:
        copy.start()
    for i, copy in enumerate(copies):
        copy.wait()
        rows = slice(i * size, (i + 1) * size)
        block = buffer[rows, :]
        high = block.astype(BF16)
        high_ref[rows, :] = high
        low_ref[rows, :] = (block - high.astype(F32)).astype(BF16)


def first_kernel(position, rhs, basis, even, odd, even_cluster, odd_cluster, v_ref, near_ref, packet_ref):
    face = rhs.shape[0] // 4
    modes = basis.shape[0]
    half = face // 2
    jump(position, rhs, (even, odd, even_cluster, odd_cluster), v_ref, face)
    sub_odd, _ = parities(position)

    def face_modes(packet):
        pieces = [packet[half + i : half + i + modes, :] for i in range(0, packet.shape[0] - half, modes)]
        return jnp.concatenate(pieces, axis=1)[:, :face]

    left, right = facing_pair(sub_odd, face_modes(even), face_modes(odd))
    zero = jnp.zeros_like(left)
    near = jnp.concatenate(
        [
            jnp.concatenate([-left, zero], axis=1),
            basis[...],
            jnp.concatenate([zero, -right], axis=1),
        ],
        axis=0,
    )
    place = lax.broadcasted_iota(jnp.int32, near.shape, 1)
    alive = jnp.logical_or(
        place < position[2], jnp.logical_and(place >= face, place < face + position[3])
    )
    near = jnp.where(alive, near, 0.0)
    near_ref[...] = near
    own = near[modes : 2 * modes]
    packet_ref[...] = jnp.zeros_like(packet_ref)
    packet_ref[: modes // 2, :] = pack(matmul(own, v_ref[: 2 * face, :]))
    packet_ref[modes // 2 :, : 3 * modes] = matmul_nt(own, near)


def modes_kernel(later, near, near_parts_ref, lift_ref):
    near_parts_ref[...] = jnp.concatenate(halves(near[...]), axis=0)
    lift_ref[...] = beside(near[...].T)


def lift_both(lift, once, twice):
    both = jnp.concatenate([once, twice], axis=1)
    first = both.astype(BF16).astype(F32)
    factor = jnp.concatenate(
        [
            jnp.concatenate([first, both - first], axis=1),
            jnp.concatenate([first, jnp.zeros_like(first)], axis=1),
        ],
        axis=0,
    ).astype(BF16)
    return narrow_once(passes(lift[...], factor))


def narrow_once(values):
    half = values.shape[1] // 2
    return values[:, :half] + values[:, half:]


def advance(u, take, put, high, low, near_parts, squared, work_u, work_y, work, y_ref, packet_ref, face, count):
    curvature = operate(u, take, put, high, low, work_u, work_y, work, y_ref, face)
    moments = passes(near_parts[...], work[...])
    packet_ref[:count, :] = pack(narrow(moments[: 2 * count] + moments[2 * count :]))
    parts = wide(squared[...])
    write_symmetric(0.5 * gram(parts, parts), curvature, packet_ref.at[count:, :])


def place_coarse(coarse, padded, modes):
    total = coarse.shape[0]
    padded[:modes, :] = jnp.zeros((modes, total), F32)
    padded[modes + total :, :] = jnp.zeros((modes, total), F32)
    padded[modes : modes + total, :] = coarse[...]


def place_blocks(offsets, position, packets, blocks, modes):
    for j, offset in enumerate(offsets):
        where = pl.ds(pl.multiple_of((position[0] ^ offset) * modes, modes), modes)
        begin = j * (3 * modes // 2) + modes // 2
        blocks[where, :] = packets[begin : begin + modes, :]


def second_kernel(
    offsets, position, packets, coarse, near_parts, lift, v0, take, put, high, low,
    r_ref, y_ref, even_ref, odd_ref, even_cluster_ref, odd_cluster_ref, packet_ref,
    moments, blocks, padded, image, work_u, work_y, work,
):
    order, columns = v0.shape
    face = order // 4
    modes = near_parts.shape[0] // 6
    total = coarse.shape[0]
    me = position[0]
    for j, offset in enumerate(offsets):
        where = pl.ds(pl.multiple_of((me ^ offset) * modes, modes), modes)
        begin = j * (3 * modes // 2)
        moments[where, :] = unpack(packets[begin : begin + modes // 2, :])
    place_blocks(offsets, position, packets, blocks, modes)
    place_coarse(coarse, padded, modes)
    image[:modes, :] = jnp.zeros((modes, columns), F32)
    image[modes + total :, :] = jnp.zeros((modes, columns), F32)
    image[modes : modes + total, :] = quick(coarse[...], moments[...])
    own = pl.ds(pl.multiple_of(me * modes, modes), 3 * modes)
    near_rows = padded[own, :]
    again = [
        quick(blocks[j * modes : (j + 1) * modes, : 3 * modes], image[j * modes : (j + 3) * modes, :])
        for j in range(total // modes)
    ]
    once = image[own, :]
    both = lift_both(lift, once, 2.0 * once - quick(near_rows, jnp.concatenate(again, axis=0)))
    r_ref[...] = v0[...]
    r_ref[: 2 * face, :] = v0[: 2 * face, :] - both[:, :columns]
    u = jnp.concatenate([v0[: 2 * face, :] - both[:, columns:], v0[2 * face :, :]], axis=0)
    advance(u, take, put, high, low, near_parts, r_ref, work_u, work_y, work, y_ref, packet_ref, face, 3 * modes // 2)
    write_faces(position, y_ref, (even_ref, odd_ref, even_cluster_ref, odd_cluster_ref), face)


def rows_kernel(offsets, position, later, packets, coarse, rows_ref, blocks, padded, product, columns_ref):
    total = coarse.shape[0]
    count = rows_ref.shape[1] // (2 * len(offsets))
    modes = 2 * count // 3
    place_blocks(offsets, position, packets, blocks, modes)
    place_coarse(coarse, padded, modes)
    for j in range(total // modes):
        rows = slice(j * modes, (j + 1) * modes)
        product[rows, :] = matmul(blocks[rows, : 3 * modes], padded[j * modes : (j + 3) * modes, :])
    once = padded[pl.ds(pl.multiple_of(position[0] * modes, modes), 3 * modes), :]
    columns_ref[...] = jnp.zeros_like(columns_ref)
    columns_ref[modes : modes + total, : 3 * modes] = once.T
    columns_ref[modes : modes + total, 3 * modes :] = (2.0 * once - matmul(once, product[...])).T
    pieces = [
        columns_ref[pl.ds(pl.multiple_of((position[0] ^ offset) * modes + begin, 16), count), :]
        for begin in (0, count)
        for offset in offsets
    ]
    rows_ref[...] = jnp.concatenate(halves(jnp.concatenate(pieces, axis=0).T), axis=0)


def coefficients(rows, parts):
    half = parts.shape[1] // 2
    moments = jnp.concatenate([parts[:, :half], parts[:, half:]], axis=0)
    return fold(passes(rows[...], beside(moments)))


def third_kernel(
    position, y1, even, odd, even_cluster, odd_cluster, parts, rows, near_parts, lift, take, put, high, low,
    h_ref, y_ref, even_ref, odd_ref, even_cluster_ref, odd_cluster_ref, packet_ref,
    v_ref, work_u, work_y, work,
):
    order, columns = y1.shape
    face = order // 4
    modes = near_parts.shape[0] // 6
    jump(position, y1, (even, odd, even_cluster, odd_cluster), v_ref, face)
    both = coefficients(rows, parts)
    both = lift_both(lift, both[: 3 * modes], both[3 * modes :])
    h_ref[...] = v_ref[...]
    h_ref[: 2 * face, :] = v_ref[: 2 * face, :] - both[:, :columns]
    u = jnp.concatenate([v_ref[: 2 * face, :] - both[:, columns:], v_ref[2 * face :, :]], axis=0)
    advance(u, take, put, high, low, near_parts, h_ref, work_u, work_y, work, y_ref, packet_ref, face, 3 * modes // 2)
    write_faces(position, y_ref, (even_ref, odd_ref, even_cluster_ref, odd_cluster_ref), face)


def stack_kernel(position, y2, even, odd, even_cluster, odd_cluster, r0, h1, basis_ref, v_ref):
    face = y2.shape[0] // 4
    jump(position, y2, (even, odd, even_cluster, odd_cluster), v_ref, face)
    columns = y2.shape[1]
    basis_ref[: 2 * columns, :] = jnp.concatenate([r0[...], h1[...]], axis=1).T
    basis_ref[2 * columns :, :] = v_ref[...].T


def spd_solve(matrix, target):
    order = matrix.shape[0]
    table = jnp.concatenate([matrix, target], axis=1)
    width = table.shape[1]
    size = 8
    lines = lax.broadcasted_iota(jnp.int32, (size, width), 0)
    rows = [table[i : i + size] for i in range(0, order, size)]
    for k in range(0, order, size):
        panel = rows[k // size]
        columns = [jnp.broadcast_to(panel[:, k + j : k + j + 1], (size, width)) for j in range(size)]
        for j in range(size):
            column = columns[j]
            inverse = 1.0 / column[j : j + 1]

            def eliminate(values):
                pivot = values[j : j + 1] * inverse
                return jnp.where(lines == j, pivot, values - column * pivot)

            panel = eliminate(panel)
            columns[j + 1 :] = [eliminate(other) for other in columns[j + 1 :]]
        for i in range(order // size):
            if i == k // size:
                continue
            values = rows[i]
            terms = [
                jnp.broadcast_to(values[:, k + j : k + j + 1], (size, width)) * panel[j : j + 1] for j in range(size)
            ]
            while len(terms) > 1:
                terms = [terms[t] + terms[t + 1] for t in range(0, len(terms), 2)]
            rows[i] = values - terms[0]
        rows[k // size] = panel
    return jnp.concatenate(rows, axis=0)[:, order:]


def step_kernel(later, grams, inverse_ref, step_ref):
    descent, curvature = read_symmetric(grams[: grams.shape[0] // 2, :])
    order = curvature.shape[0]
    row, column = grid(order)
    inverse = spd_solve(curvature, jnp.where(row == column, 1.0, 0.0))
    inverse_ref[...] = inverse
    step_ref[:order, :] = matmul(inverse, descent)
    step_ref[order:, :] = curvature


def last_kernel(
    parts, rows, near, basis, grams, inverse, step,
    solution_ref, residual_ref,
):
    columns = basis.shape[0] // 3
    order = basis.shape[1]
    face = order // 4
    own = coefficients(rows, parts)[: near.shape[0]]
    g2, g3 = read_symmetric(grams[...])
    first, g1 = step[:columns, :], step[columns:, :]
    mix = matmul(inverse[...], g2)
    last = spd_solve(g3 - matmul(g2, mix), matmul(g2, first) - g1)
    alpha = first + matmul(mix, last)
    zero = jnp.zeros_like(alpha)
    weights = jnp.concatenate(
        [
            jnp.concatenate([alpha, zero], axis=1),
            jnp.concatenate([-last, -alpha], axis=1),
            jnp.concatenate([zero, last], axis=1),
        ],
        axis=0,
    )
    both = matmul(weights.T, basis[...])
    lifted = matmul(matmul(own, last).T, near[...])
    side = lax.broadcasted_iota(jnp.int32, (columns, order), 1) // face
    answer = both[:columns]
    rest = basis[:columns, :] + both[columns:] - jnp.concatenate([lifted, jnp.zeros_like(lifted)], axis=1)
    solution_ref[...] = jnp.where(side % 2 == 0, -answer, answer)
    residual_ref[...] = jnp.where(side % 2 == 0, -rest, rest)


SMEM = pl.BlockSpec(memory_space=pltpu.SMEM)
VMEM = pl.BlockSpec(memory_space=pltpu.VMEM)
ANY = pl.BlockSpec(memory_space=pl.ANY)
HBM = pl.BlockSpec(memory_space=pltpu.HBM)


def in_hbm(value):
    return pltpu.with_memory_space_constraint(value, pltpu.HBM)


def call(kernel, name, outs, scratch, limit, *args, spaces=(), work=None):
    spaces = list(spaces)
    return pl.pallas_call(
        kernel,
        name=name,
        out_shape=[out if hasattr(out, "dtype") else jax.ShapeDtypeStruct(out, F32) for out in outs],
        in_specs=spaces + [VMEM] * (len(args) - len(spaces)),
        out_specs=[VMEM] * len(outs),
        scratch_shapes=scratch,
        cost_estimate=work and pl.CostEstimate(flops=0, transcendentals=0, bytes_accessed=work),
        compiler_params=pltpu.CompilerParams(vmem_limit_bytes=limit * 2**20),
    )(*args)


def pairs(value, axis, odd):
    peers = lax.axis_size(axis)
    low = [(i, i + 1) for i in range(odd, peers - 1, 2)]
    return lax.ppermute(value, axis, low + [(j, i) for i, j in low])


def swap(value, axis, step):
    return lax.ppermute(value, axis, [(i, i ^ step) for i in range(lax.axis_size(axis))])


def steps(axis):
    return [1 << b for b in reversed(range(lax.axis_size(axis).bit_length() - 1))]


def tie(value, others):
    return lax.optimization_barrier((value, *others))[0] if others else value


def join(blocks, total):
    pieces = [piece for piece in (blocks, total) if piece is not None]
    return jnp.concatenate(pieces, axis=0) if len(pieces) > 1 else pieces[0]


def exchange(blocks, total, axis, group, after=()):
    packet = tie(join(blocks, total), after)
    got = [swap(packet, axis, step) for step in group]
    count = 0 if blocks is None else blocks.shape[0]
    if blocks is not None:
        blocks = jnp.concatenate([blocks] + [piece[:count] for piece in got], axis=0)
    if total is not None:
        sums = [piece[count:] for piece in got]
        total = total + sums[0] if len(sums) == 1 else (total + sums[0]) + (sums[1] + sums[2])
    return blocks, total


def groups(axis):
    far = steps(axis)[:-1]
    far = [far[i : i + 2] for i in range(0, len(far), 2)]
    return [group + [sum(group)] if len(group) == 2 else group for group in far], [1]


def peer_offsets(axis):
    offsets = [0]
    for step in steps(axis):
        offsets = offsets + [offset ^ step for offset in offsets]
    return offsets


def halos(even, odd, even_cluster, odd_cluster):
    return (
        pairs(even, "sub", 0),
        pairs(odd, "sub", 1),
        pairs(even_cluster, "cluster", 0),
        pairs(odd_cluster, "cluster", 1),
    )


def shards(dual_ops, contributions, block_sizes, mult_map, coarse_basis, coarse_inverse):
    operator, rhs, sizes, slot_map = dual_ops[0, 0], contributions[0, 0], block_sizes[0, 0], mult_map[0, 0]
    basis, coarse = coarse_basis[0, 0], coarse_inverse[0]
    order, columns = rhs.shape
    face = order // 4
    half = face // 2
    modes = basis.shape[0]
    total = coarse.shape[0]
    lanes = 2 * columns
    mode_rows = -(-face // lanes) * modes
    gram_rows = columns // 2 + 8
    halo = (half, lanes)
    vector = (order, columns)
    square = jax.ShapeDtypeStruct((order, order), BF16)
    count = 3 * modes // 2

    map_row = slot_map[None, :]
    rhs, basis, map_row, *faces = call(
        start_kernel,
        "start",
        [vector, basis.shape, jax.ShapeDtypeStruct(map_row.shape, jnp.int32)] + [(half + mode_rows, lanes)] * 2 + [halo] * 2,
        [pltpu.VMEM((columns, order), F32), pltpu.SemaphoreType.DMA((3,))],
        16,
        in_hbm(rhs.T), in_hbm(basis), in_hbm(map_row),
        spaces=(HBM, HBM, HBM),
    )
    permutations = call(permutation_kernel, "permutation", [square] * 2, [], 24, map_row, work=4 * 2**20)
    position = jnp.concatenate(
        [jnp.stack([lax.axis_index("sub"), lax.axis_index("cluster")]).astype(jnp.int32), tie(sizes, (map_row,))]
    )
    received = halos(*faces)
    v0, near, packet = call(
        first_kernel,
        "first",
        [vector, (3 * modes, 2 * face), (count, lanes)],
        [],
        16,
        position, tie(rhs, permutations), basis, *received,
        spaces=(SMEM,),
    )
    operators = call(
        operator_kernel,
        "operator",
        [square] * 2,
        [pltpu.VMEM((order, order), F32), pltpu.SemaphoreType.DMA((8,))],
        32,
        in_hbm(tie(operator, (packet,))),
        spaces=(HBM,),
        work=8 * 2**20,
    )
    far, near_step = groups("sub")
    offsets = peer_offsets("sub")
    packets = packet
    for group in far:
        packets, _ = exchange(packets, None, "sub", group)
    near_parts, lift = call(
        modes_kernel,
        "modes",
        [jax.ShapeDtypeStruct((6 * modes, 2 * face), BF16), jax.ShapeDtypeStruct((2 * face, 6 * modes), BF16)],
        [],
        16,
        packets, near,
        spaces=(ANY,),
        work=2 * 2**20,
    )
    packets, _ = exchange(packets, None, "sub", near_step, operators)

    works = [pltpu.VMEM((rows, 4 * columns), BF16) for rows in (order, order, 2 * face)]
    padded = [pltpu.VMEM((total, lanes), F32), pltpu.VMEM((total + 2 * modes, total), F32)]
    sends = [halo] * 4 + [(count + gram_rows, lanes)]
    r0, y1, *faces, packet = call(
        functools.partial(second_kernel, offsets),
        "second",
        [vector, vector] + sends,
        [pltpu.VMEM((total, columns), F32)] + padded + [pltpu.VMEM((total + 2 * modes, columns), F32)] + works,
        24,
        position, packets, coarse, near_parts, lift, v0, *permutations, *operators,
        spaces=(SMEM,),
    )
    received = halos(*faces)
    parts, gram01 = packet[:count], packet[count:]
    for group in far:
        parts, gram01 = exchange(parts, gram01, "sub", group)
    (rows,) = call(
        functools.partial(rows_kernel, offsets),
        "rows",
        [jax.ShapeDtypeStruct((12 * modes, 2 * count * len(offsets)), BF16)],
        padded + [pltpu.VMEM((total, total), F32), pltpu.VMEM((total + 2 * modes, 6 * modes), F32)],
        16,
        position, parts, packets, coarse,
        spaces=(SMEM, ANY),
        work=2 * 2**20,
    )
    parts, gram01 = exchange(parts, gram01, "sub", near_step, (*received, rows))
    h1, y2, *faces, packet = call(
        third_kernel,
        "third",
        [vector, vector] + sends,
        [pltpu.VMEM(vector, F32)] + works,
        24,
        position, y1, *received, parts, rows, near_parts, lift, *permutations, *operators,
        spaces=(SMEM,),
    )
    grams = jnp.concatenate([gram01, packet[count:]], axis=0)
    received = halos(*faces)
    far = steps("cluster")
    for group in [far[i : i + 2] for i in range(0, len(far), 2)]:
        _, grams = exchange(None, grams, "cluster", group + [sum(group)] if len(group) == 2 else group)
    parts, gram23 = packet[:count], tie(grams, received[:3])[gram_rows:]
    for group in groups("sub")[0]:
        parts, gram23 = exchange(parts, gram23, "sub", group)
    (stacked,) = call(
        stack_kernel,
        "stack",
        [(3 * columns, order)],
        [pltpu.VMEM(vector, F32)],
        16,
        position, y2, *received, r0, h1,
        spaces=(SMEM,),
        work=4 * 2**20,
    )
    inverse, step0 = call(
        step_kernel,
        "step",
        [(columns, columns), (2 * columns, columns)],
        [],
        16,
        stacked, grams,
        spaces=(ANY,),
        work=4 * 2**20,
    )
    parts, gram23 = exchange(parts, gram23, "sub", near_step, (stacked, inverse))
    answer, rest = call(
        last_kernel,
        "last",
        [(columns, order)] * 2,
        [],
        16,
        parts, rows, near, stacked, gram23, inverse, step0,
    )
    return answer.T[None, None], rest.T[None, None]


def solution(mesh):
    return jax.shard_map(
        shards,
        mesh=mesh,
        in_specs=(
            P("cluster", "sub", None, None),
            P("cluster", "sub", None, None),
            P("cluster", "sub", None),
            P("cluster", "sub", None),
            P("cluster", "sub", None, None),
            P("cluster", None, None),
        ),
        out_specs=(P("cluster", "sub", None, None), P("cluster", "sub", None, None)),
        check_vma=False,
    )
```

```python
import functools

import jax
import jax.numpy as jnp
from jax import lax
from jax.experimental import pallas as pl
from jax.experimental.pallas import tpu as pltpu
from jax.sharding import PartitionSpec as P

F32 = jnp.float32
BF16 = jnp.bfloat16


def matmul(left, right):
    return jnp.dot(left, right, precision=lax.Precision.HIGHEST, preferred_element_type=F32)


def matmul_nt(left, right):
    return lax.dot_general(
        left, right, (((1,), (1,)), ((), ())), precision=lax.Precision.HIGHEST, preferred_element_type=F32
    )


def passes(left, right):
    return jnp.dot(left, right, preferred_element_type=F32)


def halves(values):
    first = values.astype(BF16)
    return first, (values - first.astype(F32)).astype(BF16)


def quick(left, right):
    return fold(passes(jnp.concatenate(halves(left), axis=0), beside(right)))


def beside(right):
    first = right.astype(BF16).astype(F32)
    return jnp.concatenate([first, right - first], axis=1).astype(BF16)


def fold(products):
    rows, columns = products.shape[0] // 2, products.shape[1] // 2
    products = products[:rows] + products[rows:]
    return products[:, :columns] + products[:, columns:]


def pack(rows):
    half = rows.shape[0] // 2
    return jnp.concatenate([rows[:half], rows[half:]], axis=1)


def unpack(packed):
    half = packed.shape[1] // 2
    return jnp.concatenate([packed[:, :half], packed[:, half:]], axis=0)


def wide(values):
    first = values.astype(BF16).astype(F32)
    rest = values - first
    second = rest.astype(BF16).astype(F32)
    third = rest - second
    return jnp.concatenate(
        [
            jnp.concatenate([first, second], axis=1).astype(BF16),
            jnp.concatenate([third, jnp.zeros_like(third)], axis=1).astype(BF16),
        ],
        axis=1,
    )


def narrow(values):
    half = values.shape[1] // 2
    values = values[:, :half] + values[:, half:]
    half = half // 2
    return values[:, :half] + values[:, half:]


def operate(u, take, put, high, low, work_u, work_y, work, y_ref, face):
    order = take.shape[0]
    blocks = [slice(begin, begin + face) for begin in range(0, order, face)]
    parts = wide(u)
    for rows in blocks:
        work_u[rows, :] = passes(take[rows, :], parts).astype(BF16)
    parts = work_u[...]
    for rows in blocks:
        work_y[rows, :] = wide(narrow(passes(high[rows, :], parts) + passes(low[rows, :], parts)))
    parts = work_y[...]
    for rows in blocks:
        placed = passes(put[rows, :], parts)
        y_ref[rows, :] = narrow(placed)
        if rows.stop <= work.shape[0]:
            work[rows, :] = placed.astype(BF16)
    return gram(work_u[...], work_y[...])


def gram(left, right):
    full = lax.dot_general(left, right, (((0,), (0,)), ((), ())), preferred_element_type=F32)
    rows = full.shape[0] // 4
    full = (full[:rows] + full[rows : 2 * rows]) + full[2 * rows : 3 * rows]
    return narrow(full)


def grid(order):
    return (
        lax.broadcasted_iota(jnp.int32, (order, order), 0),
        lax.broadcasted_iota(jnp.int32, (order, order), 1),
    )


def write_symmetric(first, second, out):
    order = first.shape[0]
    row, column = grid(order)
    half = order // 2
    out[:half, :] = pack(jnp.where(row <= column, first, second))
    diagonal = jnp.sum(jnp.where(row == column, second, 0.0), axis=0, keepdims=True)
    out[half:, :order] = jnp.broadcast_to(diagonal, (out.shape[0] - half, order))
    out[half:, order:] = jnp.zeros((out.shape[0] - half, order), F32)


def read_symmetric(packed):
    order = packed.shape[1] // 2
    row, column = grid(order)
    both = unpack(packed[: order // 2, :])
    flipped = both.T
    diagonal = packed[order // 2 : order // 2 + 1, :order]
    first = jnp.where(row <= column, both, flipped)
    second = jnp.where(row < column, flipped, jnp.where(row == column, diagonal, both))
    return first, second


def parities(position):
    return position[0] % 2, position[1] % 2


def write_faces(position, source, outs, face):
    sub_odd, cluster_odd = parities(position)
    sides = (1 - sub_odd, sub_odd, 3 - cluster_odd, 2 + cluster_odd)
    for side, out in zip(sides, outs):
        out[: face // 2, :] = pack(source[pl.ds(pl.multiple_of(side * face, 16), face), :])


def facing_pair(odd, even_pair, odd_pair):
    return jnp.where(odd == 0, odd_pair, even_pair), jnp.where(odd == 0, even_pair, odd_pair)


def jump(position, source, packets, v_ref, face):
    sub_odd, cluster_odd = parities(position)
    half = face // 2
    halos = [packet[:half, :] for packet in packets]
    facing = facing_pair(sub_odd, halos[0], halos[1]) + facing_pair(cluster_odd, halos[2], halos[3])
    place = lax.broadcasted_iota(jnp.int32, (face, source.shape[1]), 0)
    for side in range(4):
        rows = slice(side * face, (side + 1) * face)
        v_ref[rows, :] = jnp.where(place < position[2 + side], source[rows, :] - unpack(facing[side]), 0.0)


def start_kernel(
    rhs_t, basis, map_row, rhs_ref, basis_ref, map_ref, even_ref, odd_ref, even_cluster_ref, odd_cluster_ref, buffer, arrived
):
    copies = [
        pltpu.make_async_copy(rhs_t, buffer, arrived.at[0]),
        pltpu.make_async_copy(basis, basis_ref, arrived.at[1]),
        pltpu.make_async_copy(map_row, map_ref, arrived.at[2]),
    ]
    for copy in copies:
        copy.start()
    face = rhs_t.shape[1] // 4
    modes = basis.shape[0]
    position = (lax.axis_index("sub"), lax.axis_index("cluster"))
    copies[0].wait()
    rhs_ref[...] = buffer[...].T
    write_faces(position, rhs_ref, (even_ref, odd_ref, even_cluster_ref, odd_cluster_ref), face)
    copies[1].wait()
    copies[2].wait()
    sub_odd, _ = parities(position)
    lower, upper = basis_ref[:, :face], basis_ref[:, face:]
    half = face // 2
    for out, chosen in (
        (even_ref, jnp.where(sub_odd == 0, upper, lower)),
        (odd_ref, jnp.where(sub_odd == 0, lower, upper)),
    ):
        lanes = out.shape[1]
        for i, begin in enumerate(range(0, face, lanes)):
            piece = chosen[:, begin : min(begin + lanes, face)]
            if piece.shape[1] < lanes:
                piece = jnp.concatenate([piece, jnp.zeros((modes, lanes - piece.shape[1]), F32)], axis=1)
            out[half + i * modes : half + (i + 1) * modes, :] = piece


def permutation_kernel(map_row, take_ref, put_ref):
    order = map_row.shape[1]
    face = order // 4
    row = map_row[...]
    lanes = 128
    column = jnp.broadcast_to(row.astype(F32), (lanes, order)).T.astype(jnp.int32)
    lane = lax.broadcasted_iota(jnp.int32, (face, lanes), 1)
    line = lax.broadcasted_iota(jnp.int32, (face, order), 0)
    for first in range(0, order, face):
        rows = slice(first, first + face)
        for begin in range(0, order, lanes):
            take_ref[rows, begin : begin + lanes] = (column[rows] == lane + begin).astype(F32).astype(BF16)
        put_ref[rows, :] = (row == line + first).astype(F32).astype(BF16)


def operator_kernel(operator, high_ref, low_ref, buffer, arrived):
    size = buffer.shape[0] // arrived.shape[0]
    copies = [
        pltpu.make_async_copy(
            operator.at[pl.ds(i * size, size)], buffer.at[pl.ds(i * size, size)], arrived.at[i]
        )
        for i in range(arrived.shape[0])
    ]
    for copy in copies:
        copy.start()
    for i, copy in enumerate(copies):
        copy.wait()
        rows = slice(i * size, (i + 1) * size)
        block = buffer[rows, :]
        high = block.astype(BF16)
        high_ref[rows, :] = high
        low_ref[rows, :] = (block - high.astype(F32)).astype(BF16)


def first_kernel(position, rhs, basis, even, odd, even_cluster, odd_cluster, v_ref, near_ref, packet_ref):
    face = rhs.shape[0] // 4
    modes = basis.shape[0]
    half = face // 2
    jump(position, rhs, (even, odd, even_cluster, odd_cluster), v_ref, face)
    sub_odd, _ = parities(position)

    def face_modes(packet):
        pieces = [packet[half + i : half + i + modes, :] for i in range(0, packet.shape[0] - half, modes)]
        return jnp.concatenate(pieces, axis=1)[:, :face]

    left, right = facing_pair(sub_odd, face_modes(even), face_modes(odd))
    zero = jnp.zeros_like(left)
    near = jnp.concatenate(
        [
            jnp.concatenate([-left, zero], axis=1),
            basis[...],
            jnp.concatenate([zero, -right], axis=1),
        ],
        axis=0,
    )
    place = lax.broadcasted_iota(jnp.int32, near.shape, 1)
    alive = jnp.logical_or(
        place < position[2], jnp.logical_and(place >= face, place < face + position[3])
    )
    near = jnp.where(alive, near, 0.0)
    near_ref[...] = near
    own = near[modes : 2 * modes]
    packet_ref[...] = jnp.zeros_like(packet_ref)
    packet_ref[: modes // 2, :] = pack(matmul(own, v_ref[: 2 * face, :]))
    packet_ref[modes // 2 :, : 3 * modes] = matmul_nt(own, near)


def modes_kernel(later, near, near_parts_ref, lift_ref):
    near_parts_ref[...] = jnp.concatenate(halves(near[...]), axis=0)
    lift_ref[...] = beside(near[...].T)


def lift_both(lift, once, twice):
    both = jnp.concatenate([once, twice], axis=1)
    first = both.astype(BF16).astype(F32)
    factor = jnp.concatenate(
        [
            jnp.concatenate([first, both - first], axis=1),
            jnp.concatenate([first, jnp.zeros_like(first)], axis=1),
        ],
        axis=0,
    ).astype(BF16)
    return narrow_once(passes(lift[...], factor))


def narrow_once(values):
    half = values.shape[1] // 2
    return values[:, :half] + values[:, half:]


def advance(u, take, put, high, low, near_parts, squared, work_u, work_y, work, y_ref, packet_ref, face, count):
    curvature = operate(u, take, put, high, low, work_u, work_y, work, y_ref, face)
    moments = passes(near_parts[...], work[...])
    packet_ref[:count, :] = pack(narrow(moments[: 2 * count] + moments[2 * count :]))
    parts = wide(squared[...])
    write_symmetric(0.5 * gram(parts, parts), curvature, packet_ref.at[count:, :])


def place_coarse(coarse, padded, modes):
    total = coarse.shape[0]
    padded[:modes, :] = jnp.zeros((modes, total), F32)
    padded[modes + total :, :] = jnp.zeros((modes, total), F32)
    padded[modes : modes + total, :] = coarse[...]


def place_blocks(offsets, position, packets, blocks, modes):
    for j, offset in enumerate(offsets):
        where = pl.ds(pl.multiple_of((position[0] ^ offset) * modes, modes), modes)
        begin = j * (3 * modes // 2) + modes // 2
        blocks[where, :] = packets[begin : begin + modes, :]


def second_kernel(
    offsets, position, packets, coarse, near_parts, lift, v0, take, put, high, low,
    r_ref, y_ref, even_ref, odd_ref, even_cluster_ref, odd_cluster_ref, packet_ref,
    moments, blocks, padded, image, work_u, work_y, work,
):
    order, columns = v0.shape
    face = order // 4
    modes = near_parts.shape[0] // 6
    total = coarse.shape[0]
    me = position[0]
    for j, offset in enumerate(offsets):
        where = pl.ds(pl.multiple_of((me ^ offset) * modes, modes), modes)
        begin = j * (3 * modes // 2)
        moments[where, :] = unpack(packets[begin : begin + modes // 2, :])
    place_blocks(offsets, position, packets, blocks, modes)
    place_coarse(coarse, padded, modes)
    image[:modes, :] = jnp.zeros((modes, columns), F32)
    image[modes + total :, :] = jnp.zeros((modes, columns), F32)
    image[modes : modes + total, :] = quick(coarse[...], moments[...])
    own = pl.ds(pl.multiple_of(me * modes, modes), 3 * modes)
    near_rows = padded[own, :]
    again = [
        quick(blocks[j * modes : (j + 1) * modes, : 3 * modes], image[j * modes : (j + 3) * modes, :])
        for j in range(total // modes)
    ]
    once = image[own, :]
    both = lift_both(lift, once, 2.0 * once - quick(near_rows, jnp.concatenate(again, axis=0)))
    r_ref[...] = v0[...]
    r_ref[: 2 * face, :] = v0[: 2 * face, :] - both[:, :columns]
    u = jnp.concatenate([v0[: 2 * face, :] - both[:, columns:], v0[2 * face :, :]], axis=0)
    advance(u, take, put, high, low, near_parts, r_ref, work_u, work_y, work, y_ref, packet_ref, face, 3 * modes // 2)
    write_faces(position, y_ref, (even_ref, odd_ref, even_cluster_ref, odd_cluster_ref), face)


def rows_kernel(offsets, position, later, packets, coarse, rows_ref, blocks, padded, product, columns_ref):
    total = coarse.shape[0]
    count = rows_ref.shape[1] // (2 * len(offsets))
    modes = 2 * count // 3
    place_blocks(offsets, position, packets, blocks, modes)
    place_coarse(coarse, padded, modes)
    for j in range(total // modes):
        rows = slice(j * modes, (j + 1) * modes)
        product[rows, :] = matmul(blocks[rows, : 3 * modes], padded[j * modes : (j + 3) * modes, :])
    once = padded[pl.ds(pl.multiple_of(position[0] * modes, modes), 3 * modes), :]
    columns_ref[...] = jnp.zeros_like(columns_ref)
    columns_ref[modes : modes + total, : 3 * modes] = once.T
    columns_ref[modes : modes + total, 3 * modes :] = (2.0 * once - matmul(once, product[...])).T
    pieces = [
        columns_ref[pl.ds(pl.multiple_of((position[0] ^ offset) * modes + begin, 16), count), :]
        for begin in (0, count)
        for offset in offsets
    ]
    rows_ref[...] = jnp.concatenate(halves(jnp.concatenate(pieces, axis=0).T), axis=0)


def coefficients(rows, parts):
    half = parts.shape[1] // 2
    moments = jnp.concatenate([parts[:, :half], parts[:, half:]], axis=0)
    return fold(passes(rows[...], beside(moments)))


def jump_kernel(position, y1, even_cluster, odd_cluster, odd, even, v_ref):
    jump(position, y1, (even, odd, even_cluster, odd_cluster), v_ref, y1.shape[0] // 4)


def third_kernel(
    position, v_ref, parts, rows, near_parts, lift, take, put, high, low,
    h_ref, y_ref, even_ref, odd_ref, even_cluster_ref, odd_cluster_ref, packet_ref,
    work_u, work_y, work,
):
    order, columns = v_ref.shape
    face = order // 4
    modes = near_parts.shape[0] // 6
    both = coefficients(rows, parts)
    both = lift_both(lift, both[: 3 * modes], both[3 * modes :])
    h_ref[...] = v_ref[...]
    h_ref[: 2 * face, :] = v_ref[: 2 * face, :] - both[:, :columns]
    u = jnp.concatenate([v_ref[: 2 * face, :] - both[:, columns:], v_ref[2 * face :, :]], axis=0)
    advance(u, take, put, high, low, near_parts, h_ref, work_u, work_y, work, y_ref, packet_ref, face, 3 * modes // 2)
    write_faces(position, y_ref, (even_ref, odd_ref, even_cluster_ref, odd_cluster_ref), face)


def stack_kernel(position, y2, even, odd, even_cluster, odd_cluster, r0, h1, basis_ref, v_ref):
    face = y2.shape[0] // 4
    jump(position, y2, (even, odd, even_cluster, odd_cluster), v_ref, face)
    columns = y2.shape[1]
    basis_ref[: 2 * columns, :] = jnp.concatenate([r0[...], h1[...]], axis=1).T
    basis_ref[2 * columns :, :] = v_ref[...].T


def spd_solve(matrix, target):
    order = matrix.shape[0]
    table = jnp.concatenate([matrix, target], axis=1)
    width = table.shape[1]
    size = 8
    lines = lax.broadcasted_iota(jnp.int32, (size, width), 0)
    rows = [table[i : i + size] for i in range(0, order, size)]
    for k in range(0, order, size):
        panel = rows[k // size]
        columns = [jnp.broadcast_to(panel[:, k + j : k + j + 1], (size, width)) for j in range(size)]
        for j in range(size):
            column = columns[j]
            inverse = 1.0 / column[j : j + 1]

            def eliminate(values):
                pivot = values[j : j + 1] * inverse
                return jnp.where(lines == j, pivot, values - column * pivot)

            panel = eliminate(panel)
            columns[j + 1 :] = [eliminate(other) for other in columns[j + 1 :]]
        for i in range(order // size):
            if i == k // size:
                continue
            values = rows[i]
            terms = [
                jnp.broadcast_to(values[:, k + j : k + j + 1], (size, width)) * panel[j : j + 1] for j in range(size)
            ]
            while len(terms) > 1:
                terms = [terms[t] + terms[t + 1] for t in range(0, len(terms), 2)]
            rows[i] = values - terms[0]
        rows[k // size] = panel
    return jnp.concatenate(rows, axis=0)[:, order:]


def step_kernel(later, grams, inverse_ref, step_ref):
    descent, curvature = read_symmetric(grams[: grams.shape[0] // 2, :])
    order = curvature.shape[0]
    row, column = grid(order)
    inverse = spd_solve(curvature, jnp.where(row == column, 1.0, 0.0))
    inverse_ref[...] = inverse
    step_ref[:order, :] = matmul(inverse, descent)
    step_ref[order:, :] = curvature


def last_kernel(
    parts, rows, near, basis, grams, inverse, step,
    solution_ref, residual_ref,
):
    columns = basis.shape[0] // 3
    order = basis.shape[1]
    face = order // 4
    own = coefficients(rows, parts)[: near.shape[0]]
    g2, g3 = read_symmetric(grams[...])
    first, g1 = step[:columns, :], step[columns:, :]
    mix = matmul(inverse[...], g2)
    last = spd_solve(g3 - matmul(g2, mix), matmul(g2, first) - g1)
    alpha = first + matmul(mix, last)
    zero = jnp.zeros_like(alpha)
    weights = jnp.concatenate(
        [
            jnp.concatenate([alpha, zero], axis=1),
            jnp.concatenate([-last, -alpha], axis=1),
            jnp.concatenate([zero, last], axis=1),
        ],
        axis=0,
    )
    both = matmul(weights.T, basis[...])
    lifted = matmul(matmul(own, last).T, near[...])
    side = lax.broadcasted_iota(jnp.int32, (columns, order), 1) // face
    answer = both[:columns]
    rest = basis[:columns, :] + both[columns:] - jnp.concatenate([lifted, jnp.zeros_like(lifted)], axis=1)
    solution_ref[...] = jnp.where(side % 2 == 0, -answer, answer)
    residual_ref[...] = jnp.where(side % 2 == 0, -rest, rest)


SMEM = pl.BlockSpec(memory_space=pltpu.SMEM)
VMEM = pl.BlockSpec(memory_space=pltpu.VMEM)
ANY = pl.BlockSpec(memory_space=pl.ANY)
HBM = pl.BlockSpec(memory_space=pltpu.HBM)


def in_hbm(value):
    return pltpu.with_memory_space_constraint(value, pltpu.HBM)


def call(kernel, name, outs, scratch, limit, *args, spaces=(), work=None):
    spaces = list(spaces)
    return pl.pallas_call(
        kernel,
        name=name,
        out_shape=[out if hasattr(out, "dtype") else jax.ShapeDtypeStruct(out, F32) for out in outs],
        in_specs=spaces + [VMEM] * (len(args) - len(spaces)),
        out_specs=[VMEM] * len(outs),
        scratch_shapes=scratch,
        cost_estimate=work and pl.CostEstimate(flops=0, transcendentals=0, bytes_accessed=work),
        compiler_params=pltpu.CompilerParams(vmem_limit_bytes=limit * 2**20),
    )(*args)


def pairs(value, axis, odd):
    peers = lax.axis_size(axis)
    low = [(i, i + 1) for i in range(odd, peers - 1, 2)]
    return lax.ppermute(value, axis, low + [(j, i) for i, j in low])


def swap(value, axis, step):
    return lax.ppermute(value, axis, [(i, i ^ step) for i in range(lax.axis_size(axis))])


def steps(axis):
    return [1 << b for b in reversed(range(lax.axis_size(axis).bit_length() - 1))]


def tie(value, others):
    return lax.optimization_barrier((value, *others))[0] if others else value


def join(blocks, total):
    pieces = [piece for piece in (blocks, total) if piece is not None]
    return jnp.concatenate(pieces, axis=0) if len(pieces) > 1 else pieces[0]


def exchange(blocks, total, axis, group, after=()):
    packet = tie(join(blocks, total), after)
    got = [swap(packet, axis, step) for step in group]
    count = 0 if blocks is None else blocks.shape[0]
    if blocks is not None:
        blocks = jnp.concatenate([blocks] + [piece[:count] for piece in got], axis=0)
    if total is not None:
        sums = [piece[count:] for piece in got]
        total = total + sums[0] if len(sums) == 1 else (total + sums[0]) + (sums[1] + sums[2])
    return blocks, total


def groups(axis):
    far = steps(axis)[:-1]
    far = [far[i : i + 2] for i in range(0, len(far), 2)]
    return [group + [sum(group)] if len(group) == 2 else group for group in far], [1]


def peer_offsets(axis):
    offsets = [0]
    for step in steps(axis):
        offsets = offsets + [offset ^ step for offset in offsets]
    return offsets


def halos(even, odd, even_cluster, odd_cluster):
    even_cluster, odd_cluster = pairs(even_cluster, "cluster", 0), pairs(odd_cluster, "cluster", 1)
    odd, even = pairs(odd, "sub", 1), pairs(even, "sub", 0)
    return even, odd, even_cluster, odd_cluster


def shards(dual_ops, contributions, block_sizes, mult_map, coarse_basis, coarse_inverse):
    operator, rhs, sizes, slot_map = dual_ops[0, 0], contributions[0, 0], block_sizes[0, 0], mult_map[0, 0]
    basis, coarse = coarse_basis[0, 0], coarse_inverse[0]
    order, columns = rhs.shape
    face = order // 4
    half = face // 2
    modes = basis.shape[0]
    total = coarse.shape[0]
    lanes = 2 * columns
    mode_rows = -(-face // lanes) * modes
    gram_rows = columns // 2 + 8
    halo = (half, lanes)
    vector = (order, columns)
    square = jax.ShapeDtypeStruct((order, order), BF16)
    count = 3 * modes // 2

    map_row = slot_map[None, :]
    rhs, basis, map_row, *faces = call(
        start_kernel,
        "start",
        [vector, basis.shape, jax.ShapeDtypeStruct(map_row.shape, jnp.int32)] + [(half + mode_rows, lanes)] * 2 + [halo] * 2,
        [pltpu.VMEM((columns, order), F32), pltpu.SemaphoreType.DMA((3,))],
        16,
        in_hbm(rhs.T), in_hbm(basis), in_hbm(map_row),
        spaces=(HBM, HBM, HBM),
    )
    permutations = call(permutation_kernel, "permutation", [square] * 2, [], 24, map_row, work=4 * 2**20)
    position = jnp.concatenate(
        [jnp.stack([lax.axis_index("sub"), lax.axis_index("cluster")]).astype(jnp.int32), tie(sizes, (map_row,))]
    )
    received = halos(*faces)
    v0, near, packet = call(
        first_kernel,
        "first",
        [vector, (3 * modes, 2 * face), (count, lanes)],
        [],
        16,
        position, tie(rhs, permutations), basis, *received,
        spaces=(SMEM,),
    )
    operators = call(
        operator_kernel,
        "operator",
        [square] * 2,
        [pltpu.VMEM((order, order), F32), pltpu.SemaphoreType.DMA((8,))],
        32,
        in_hbm(tie(operator, (packet,))),
        spaces=(HBM,),
        work=8 * 2**20,
    )
    far, near_step = groups("sub")
    offsets = peer_offsets("sub")
    packets = packet
    for group in far:
        packets, _ = exchange(packets, None, "sub", group)
    near_parts, lift = call(
        modes_kernel,
        "modes",
        [jax.ShapeDtypeStruct((6 * modes, 2 * face), BF16), jax.ShapeDtypeStruct((2 * face, 6 * modes), BF16)],
        [],
        16,
        packets, near,
        spaces=(ANY,),
        work=2 * 2**20,
    )
    packets, _ = exchange(packets, None, "sub", near_step, operators)

    works = [pltpu.VMEM((rows, 4 * columns), BF16) for rows in (order, order, 2 * face)]
    padded = [pltpu.VMEM((total, lanes), F32), pltpu.VMEM((total + 2 * modes, total), F32)]
    sends = [halo] * 4 + [(count + gram_rows, lanes)]
    r0, y1, *faces, packet = call(
        functools.partial(second_kernel, offsets),
        "second",
        [vector, vector] + sends,
        [pltpu.VMEM((total, columns), F32)] + padded + [pltpu.VMEM((total + 2 * modes, columns), F32)] + works,
        24,
        position, packets, coarse, near_parts, lift, v0, *permutations, *operators,
        spaces=(SMEM,),
    )
    received = halos(*faces)
    parts, gram01 = packet[:count], packet[count:]
    for group in far:
        parts, gram01 = exchange(parts, gram01, "sub", group)
    (rows,) = call(
        functools.partial(rows_kernel, offsets),
        "rows",
        [jax.ShapeDtypeStruct((12 * modes, 2 * count * len(offsets)), BF16)],
        padded + [pltpu.VMEM((total, total), F32), pltpu.VMEM((total + 2 * modes, 6 * modes), F32)],
        16,
        position, parts, packets, coarse,
        spaces=(SMEM, ANY),
        work=2 * 2**20,
    )
    parts, gram01 = exchange(parts, gram01, "sub", near_step, (*received[2:], *received[1::-1], rows))
    (v1,) = call(jump_kernel, "jump", [vector], [], 16, position, y1, *received[2:], *received[1::-1], spaces=(SMEM,), work=2 * 2**20)
    h1, y2, *faces, packet = call(
        third_kernel,
        "third",
        [vector, vector] + sends,
        works,
        24,
        position, v1, parts, rows, near_parts, lift, *permutations, *operators,
        spaces=(SMEM,),
    )
    grams = jnp.concatenate([gram01, packet[count:]], axis=0)
    received = halos(*faces)
    far = steps("cluster")
    for group in [far[i : i + 2] for i in range(0, len(far), 2)]:
        _, grams = exchange(None, grams, "cluster", group + [sum(group)] if len(group) == 2 else group)
    parts, gram23 = packet[:count], tie(grams, received[:3])[gram_rows:]
    for group in groups("sub")[0]:
        parts, gram23 = exchange(parts, gram23, "sub", group)
    (stacked,) = call(
        stack_kernel,
        "stack",
        [(3 * columns, order)],
        [pltpu.VMEM(vector, F32)],
        16,
        position, y2, *received, r0, h1,
        spaces=(SMEM,),
        work=4 * 2**20,
    )
    inverse, step0 = call(
        step_kernel,
        "step",
        [(columns, columns), (2 * columns, columns)],
        [],
        16,
        stacked, grams,
        spaces=(ANY,),
        work=4 * 2**20,
    )
    parts, gram23 = exchange(parts, gram23, "sub", near_step, (stacked, inverse))
    answer, rest = call(
        last_kernel,
        "last",
        [(columns, order)] * 2,
        [],
        16,
        parts, rows, near, stacked, gram23, inverse, step0,
    )
    return answer.T[None, None], rest.T[None, None]


def solution(mesh):
    return jax.shard_map(
        shards,
        mesh=mesh,
        in_specs=(
            P("cluster", "sub", None, None),
            P("cluster", "sub", None, None),
            P("cluster", "sub", None),
            P("cluster", "sub", None),
            P("cluster", "sub", None, None),
            P("cluster", None, None),
        ),
        out_specs=(P("cluster", "sub", None, None), P("cluster", "sub", None, None)),
        check_vma=False,
    )
```
